512 devices in a mesh: tile: 128 (over z, y, core), frame: 4 (over x).
Axes of the slice: x: 4, y: 8, z: 8, core: 2. Of those that a mesh axis runs over, the one named last changes fastest.
Arguments:
- recording: bfloat16 [131072, 512], P('tile', 'frame'), may hold values from 0 to 2
- footprints: bfloat16 [131072, 128], P('tile'), may hold values from 0 to 10, as said below
- slot_owner: int32 [16384, 1], P('tile'), may hold values from 0 to 127; in each aligned block of 128 rows (0 to 127, 128 to 255, ...) at most 2 rows name the same one
- slot_pick: int32 [16384], P('tile'), may hold values from 0 to 39
- traces: float32 [40960, 512], P('tile', 'frame'), may hold values from 0 to 1
Outputs:
- new_traces: float32 [40960, 512], P('tile', 'frame')
- new_footprints: bfloat16 [131072, 128], P('tile')
The draws below stay inside these ranges and needn't reach their ends.
Inputs may be any that keep to these rules, and one draw needn't show every extreme that they name: `footprints`: nonnegative; a slot's nonzero entries mark its footprint's support, all other entries are exactly zero. `slot_owner`: of the 128 slots of one tile no owner is named by more than 2, a bound that some block reaches.
All inputs are finite; a program needn't handle non-finite values.
Results may differ from the reference program's by a relative error of at most 0.003.
Values may be sent and summed in bfloat16 or wider, within the bound.
A program may use at most 64 MiB of HBM per device.

```python
import math
import jax
import jax.numpy as jnp
import numpy as np
from jax import lax

K = 128
NO = 320
V_DEV = 1024
ITER_C = 4
ITER_A = 8
CAP = 2
VOXELS = 131072
FRAMES = 512
NEUR = 40960
SLOTS = 16384
N_TILE = 128


def draw_footprints(key, part):
    key_start, key_length, key_value, key_scale = jax.random.split(key, 4)
    start_cell = jax.random.randint(key_start, (N_TILE, 1, K), 0, V_DEV)
    run_length = jax.random.randint(key_length, (N_TILE, 1, K), V_DEV // 8, V_DEV // 2 + 1)
    voxel_index = jnp.arange(V_DEV, dtype=jnp.int32)[None, :, None]
    offset = (voxel_index - start_cell) % V_DEV
    support = offset < run_length
    values = jax.random.uniform(key_value, (N_TILE, V_DEV, K), jnp.float32, 0.2, 1.0)
    column_scale = jnp.exp(jax.random.uniform(key_scale, (N_TILE, 1, K), jnp.float32, 0.0, math.log(10.0)))
    values = values * column_scale
    return jnp.where(support, values, 0.0).reshape(VOXELS, K).astype(jnp.bfloat16)


def draw_traces(key, part):
    values = jax.random.uniform(jax.random.fold_in(key, 7), (NEUR, FRAMES), jnp.float32, 0.0, 1.0)
    local_index = jnp.arange(NEUR, dtype=jnp.int32) % NO
    active = local_index < max(2, NO // 8)
    level = jnp.where(active, 1.0, 0.1).astype(jnp.float32)
    return (values * level[:, None]).astype(jnp.float32)


def plant(array, stream_key, least, high):
    index_at = [jax.random.randint(jax.random.fold_in(stream_key, axis), (), 0, length) for axis, length in enumerate(array.shape)]
    widest = array.shape.index(max(array.shape))
    neighbour = index_at[:widest] + [(index_at[widest] + 1) % array.shape[widest]] + index_at[widest + 1:]
    return array.at[tuple(index_at)].set(least).at[tuple(neighbour)].set(high)


def shard_levels(rng, shape, cuts, low, top_value):
    def one(axis_at, shards_of):
        steps = jax.random.uniform(jax.random.fold_in(jax.random.fold_in(rng, 6), axis_at), (shards_of,), jnp.float32, low / len(cuts), top_value / len(cuts))
        return jnp.repeat(jnp.exp(steps), shape[axis_at] // shards_of).reshape((-1,) + (1,) * (len(shape) - axis_at - 1))

    loudness = one(*cuts[0])
    for cut in cuts[1:]:
        loudness = loudness * one(*cut)
    return loudness


def routed_block(key, own, number, rows, number_of, top, bound, lean):
    sequence = jax.random.permutation(key, number_of)
    crowded, usual = portions_of(number_of, rows * top, bound, lean, True), portions_of(number_of, rows * top, bound, lean, False)
    places = jnp.arange(number_of)

    def named(sizes, turn):
        used = int((sizes > 0).sum())
        fixed = max(1, used // 4)
        moved = fixed + (places - fixed + turn * (used - fixed)) % max(1, number_of - fixed)
        return jnp.zeros((number_of,), jnp.int32).at[sequence[jnp.where(places < fixed, places, moved)]].set(jnp.asarray(sizes, jnp.int32))

    sizes = jnp.where(number % 4 == 0, named(crowded, number // 4), named(usual, number - number // 4 - 1))
    mixed = jax.random.permutation(jax.random.fold_in(own, 3), number_of)
    source_of, sink = mixed[0:number_of // 2 * 2:2], mixed[1:number_of // 2 * 2:2]
    slack = jnp.minimum(sizes[source_of] - 1, bound - sizes[sink]) // 2
    slack = jnp.where((source_of == sequence[0]) | (sink == sequence[0]) | (sizes[sink] == 0), 0, jnp.maximum(slack, 0))
    moved = jax.random.randint(jax.random.fold_in(own, 4), (number_of // 2,), 0, 1 << 20) % (slack + 1)
    sizes = sizes.at[source_of].add(-moved).at[sink].add(moved)
    members = jnp.searchsorted(jnp.cumsum(sizes), jnp.arange(rows * top), side="right").astype(jnp.int32)
    listing = members.reshape(top, rows).T
    listing = listing[jax.random.permutation(jax.random.fold_in(own, 1), rows)]
    turn = jax.random.randint(jax.random.fold_in(own, 2), (rows, 1), 0, top)
    return jnp.take_along_axis(listing, (jnp.arange(top)[None, :] + turn) % top, axis=1)


def portions_of(count, total, most, lean, full):
    loads = [(1 << 20) // math.isqrt(standing ** lean) + 1 for standing in range(1, count + 1)]
    largest = most if full else min(most, max(-(-total // count), total * loads[0] // sum(loads)))
    least = 1 if total - largest >= count - 1 else 0
    given, rest = [largest] + [least] * (count - 1), total - largest - least * (count - 1)
    while rest > 0:
        movable = [i for i in range(1, count) if given[i] < largest] or [i for i in range(1, count) if given[i] < most]
        mass, left = sum([loads[i] for i in movable]), rest
        for i in movable:
            more = min(most - given[i], max(1, left * loads[i] // mass), rest)
            given[i] = given[i] + more
            rest = rest - more
    return np.array(given)


def setup_inputs(seed: int = 0) -> dict:
    keys = jax.random.split(jax.random.key(seed), 6)
    recording = jnp.clip(2.0 * jax.random.uniform(keys[0], (VOXELS, FRAMES), jnp.float32) ** shard_levels(keys[0], (VOXELS, FRAMES), ((0, 128), (1, 4)), -0.2, 0.2), 0.0, 2.0).astype(jnp.bfloat16)
    footprints = draw_footprints(jax.random.fold_in(keys[5], 71), 0)
    slot_owner_keys = jax.random.split(jax.random.fold_in(keys[2], 1), SLOTS // K)
    slot_owner_turns = jax.random.permutation(jax.random.fold_in(keys[2], 3), SLOTS // K)
    slot_owner = jax.vmap(lambda own, number: routed_block(jax.random.fold_in(keys[2], 2), own, number, K, N_TILE, 1, CAP, 2))(slot_owner_keys, slot_owner_turns).reshape((SLOTS, 1))
    slot_pick = plant(jax.random.randint(keys[3], (SLOTS,), 0, max(2, NO // 8)), jax.random.fold_in(keys[3], 1), 0, (max(2, NO // 8)) - 1).astype(jnp.int32)
    traces = draw_traces(jax.random.fold_in(keys[5], 71), 0)
    return dict(recording=recording, footprints=footprints, slot_owner=slot_owner, slot_pick=slot_pick, traces=traces)


def tile_stats(pair):
    block, data = pair
    gram = lax.dot_general(block, block, (((0,), (0,)), ((), ())), preferred_element_type=jnp.float32)
    drive = lax.dot_general(block, data, (((0,), (0,)), ((), ())), preferred_element_type=jnp.float32)
    return gram, drive


def footprint_steps(triple):
    block, data, slot_traces = triple
    slot_low = slot_traces.astype(jnp.bfloat16)
    data_sum = lax.dot_general(data, slot_low, (((1,), (1,)), ((), ())), preferred_element_type=jnp.float32)
    trace_gram = jnp.dot(slot_traces, slot_traces.T, precision=lax.Precision.HIGHEST)
    column_step = 1.0 / (1.0 + jnp.sum(jnp.abs(trace_gram), axis=1))
    support = block > 0
    iterate = block.astype(jnp.float32)
    for sweep in range(ITER_A):
        moved = iterate - (jnp.dot(iterate, trace_gram, precision=lax.Precision.HIGHEST) - data_sum) * column_step[None, :]
        iterate = jnp.where(support, jnp.maximum(moved, 0.0), jnp.zeros_like(moved))
    return iterate.astype(jnp.bfloat16)


def reference(recording, footprints, slot_owner, slot_pick, traces):
    neuron_row = (slot_owner[:, 0] * NO + slot_pick).astype(jnp.int32)
    blocks = footprints.reshape(N_TILE, V_DEV, K)
    datas = recording.reshape(N_TILE, V_DEV, FRAMES)
    gram, drive = lax.map(tile_stats, (blocks, datas))
    row_bound = jnp.sum(jnp.abs(gram), axis=2).reshape(-1)
    bound_sum = jax.ops.segment_sum(row_bound, neuron_row, num_segments=NEUR)
    scale_row = 1.0 / (1.0 + bound_sum)
    current = traces
    for iteration in range(ITER_C):
        slot_traces = current[neuron_row].reshape(N_TILE, K, FRAMES)
        terms = jnp.einsum("tkj,tjf->tkf", gram, slot_traces, precision=lax.Precision.HIGHEST) - drive
        grad_sum = jax.ops.segment_sum(terms.reshape(SLOTS, FRAMES), neuron_row, num_segments=NEUR)
        current = jnp.maximum(current - grad_sum * scale_row[:, None], 0.0)
    slot_traces = current[neuron_row].reshape(N_TILE, K, FRAMES)
    updated = lax.map(footprint_steps, (blocks, datas, slot_traces))
    return current, updated.reshape(VOXELS, K)
```

```python
import jax
import jax.numpy as jnp
from jax import lax
from jax.experimental import pallas as pl
from jax.experimental.pallas import tpu as pltpu
from jax.sharding import PartitionSpec as P

ITER_C = 4
ITER_A = 8


def in_one_piece(arrays, axis, split_dim, concat_dim, along):
    widths = [a.shape[along] for a in arrays]
    both = jnp.concatenate(arrays, axis=along)
    whole = lax.all_to_all(both, axis, split_axis=split_dim, concat_axis=concat_dim, tiled=True)
    return tuple(jnp.split(whole, [sum(widths[:k]) for k in range(1, len(widths))], axis=along))


def side_by_side(arrays, axis, split_dim, concat_dim, along):
    columns = [a.reshape(*a.shape[:along], -1) for a in arrays]
    both = jnp.concatenate(columns, axis=along)
    whole, at, done = (
        lax.all_to_all(both, axis, split_axis=split_dim, concat_axis=concat_dim, tiled=True),
        0,
        [],
    )
    for a, column in zip(arrays, columns):
        piece = whole[..., at : at + column.shape[along]]
        done.append(piece.reshape(*piece.shape[:along], *a.shape[along:]))
        at += column.shape[along]
    return tuple(done)


def in_blocks(shard, dim, size):
    dims = shard.shape
    blocks = shard.reshape(*dims[:dim], size, dims[dim] // size, *dims[dim + 1 :])
    return jnp.moveaxis(blocks, dim, 0)


def sum_at_owner(shard, axis, dim):
    blocks = in_blocks(shard, dim, lax.axis_size(axis))
    arrived = lax.all_to_all(blocks, axis, split_axis=0, concat_axis=0, tiled=True)
    return arrived.sum(axis=0)


def sent_to_all(shard, axis):
    copies = jnp.broadcast_to(shard, (lax.axis_size(axis), *shard.shape))
    return lax.all_to_all(copies, axis, split_axis=0, concat_axis=0, tiled=True)


def over_copies(shard, axis):
    return sent_to_all(shard, axis).sum(axis=0)


def laid_out(blocks, dim):
    blocks = jnp.moveaxis(blocks, 0, dim)
    dims = blocks.shape
    return blocks.reshape(*dims[:dim], dims[dim] * dims[dim + 1], *dims[dim + 2 :])


def gathered_copies(shard, axis, dim):
    return laid_out(sent_to_all(shard, axis), dim)


def spread_rows(values, buffer_row, tile_count, capacity):
    filled = (
        jnp.zeros((tile_count * capacity,) + values.shape[1:], values.dtype)
        .at[buffer_row]
        .set(values)
    )
    return filled.reshape((tile_count, capacity) + values.shape[1:])


MESH = pl.DeviceIdType.MESH


def touch(x_ref, i_ref, o_ref, a, b, w, ss, rs):
    me = lax.axis_index("tile")
    fr = lax.axis_index("frame")
    bar = pltpu.get_barrier_semaphore()
    other = me + 1 - 2 * lax.rem(me, 2)
    pl.semaphore_signal(bar, inc=1, device_id=(other, fr), device_id_type=MESH)
    pl.semaphore_wait(bar, 1)
    a[...] = x_ref[...]
    h = pltpu.make_async_remote_copy(
        src_ref=a.at[pl.ds(pl.multiple_of(lax.rem(me, 2) * 4, 4), 4)],
        dst_ref=b.at[pl.ds(pl.multiple_of(lax.rem(me, 2) * 4, 4), 4)],
        send_sem=ss, recv_sem=rs, device_id=(other, fr), device_id_type=MESH)
    h.start()
    h.wait()
    v = a[pl.ds(0, 8, stride=4), :]
    idx = i_ref[...]
    g = jnp.take_along_axis(v, idx, axis=1)
    k = jnp.take_along_axis(g, jnp.bitwise_and(idx, 7), axis=0)
    t = jnp.transpose(jnp.concatenate([k] * 16, axis=0))
    w[...] = t
    w[pl.ds(0, 8, stride=4), :] = k
    c = jnp.where(jnp.abs(jnp.sum(w[...])) < 0.0, 1.0, 0.0) + jnp.dot(t.astype(jnp.bfloat16), w[...].astype(jnp.bfloat16), preferred_element_type=jnp.float32) * 0.0
    o_ref[...] = x_ref[...] + c[0:64, :] * 0.0


def touched(x, i):
    return pl.pallas_call(
        touch,
        out_shape=jax.ShapeDtypeStruct((64, 128), jnp.float32),
        in_specs=[pl.BlockSpec(memory_space=pltpu.VMEM)] * 2,
        out_specs=pl.BlockSpec(memory_space=pltpu.VMEM),
        scratch_shapes=[pltpu.VMEM((64, 128), jnp.float32), pltpu.VMEM((64, 128), jnp.float32), pltpu.VMEM((128, 128), jnp.float32),
                        pltpu.SemaphoreType.DMA, pltpu.SemaphoreType.DMA],
        compiler_params=pltpu.CompilerParams(collective_id=0, has_side_effects=True, vmem_limit_bytes=30 << 20),
    )(x, i)


def body(recording, footprints, slot_owner, slot_pick, traces):
    tile_count = lax.axis_size("tile")
    slot_count = footprints.shape[1]
    owned_count = traces.shape[0]
    frame_count = traces.shape[1]
    capacity = max(2, 2 * slot_count // tile_count)
    buffer_size = tile_count * capacity
    owner_tile = slot_owner[:, 0]
    position = jnp.arange(slot_count, dtype=jnp.int32)
    earlier = (owner_tile[:, None] == owner_tile[None, :]) & (position[None, :] < position[:, None])
    slot_rank = jnp.sum(earlier.astype(jnp.int32), axis=1)
    buffer_row = owner_tile * capacity + slot_rank
    want_index = spread_rows(slot_pick, buffer_row, tile_count, capacity)
    want_valid = spread_rows(jnp.ones((slot_count,), jnp.int32), buffer_row, tile_count, capacity)
    got_index, got_valid = in_one_piece((want_index, want_valid), "tile", 0, 0, 1)
    owned_index = jnp.arange(owned_count, dtype=jnp.int32)
    select = (
        (got_index.reshape(-1)[:, None] == owned_index[None, :])
        & (got_valid.reshape(-1)[:, None] == 1)
    ).astype(jnp.float32)
    slot_gram = lax.dot_general(
        footprints, footprints, (((0,), (0,)), ((), ())), preferred_element_type=jnp.float32
    )
    data_drive = lax.dot_general(
        footprints, recording, (((0,), (0,)), ((), ())), preferred_element_type=jnp.float32
    )
    row_bound = jnp.sum(jnp.abs(slot_gram), axis=1)
    head = touched(traces[:64], jnp.broadcast_to(slot_pick[None, :], (8, 128)))
    traces = jnp.concatenate([head, traces[64:]], axis=0)
    current = traces
    scale_row = jnp.ones((owned_count,), jnp.float32)
    slot_traces = traces[:slot_count]
    for iteration in range(ITER_C + 1):
        asked = jnp.dot(select, current, precision=lax.Precision.HIGHEST).reshape(
            tile_count, capacity, frame_count
        )
        arrived = lax.all_to_all(asked, "tile", split_axis=0, concat_axis=0, tiled=True)
        slot_traces = jnp.take(arrived.reshape(buffer_size, frame_count), buffer_row, axis=0)
        if iteration < ITER_C:
            slot_terms = (
                jnp.dot(slot_gram, slot_traces, precision=lax.Precision.HIGHEST) - data_drive
            )
            if iteration == 0:
                got_terms, got_bound = side_by_side(
                    (
                        spread_rows(slot_terms, buffer_row, tile_count, capacity),
                        spread_rows(row_bound, buffer_row, tile_count, capacity),
                    ),
                    "tile",
                    0,
                    0,
                    2,
                )
                bound_sum = jnp.dot(got_bound.reshape(-1), select, precision=lax.Precision.HIGHEST)
                scale_row = 1.0 / (1.0 + bound_sum)
            else:
                got_terms = lax.all_to_all(
                    spread_rows(slot_terms, buffer_row, tile_count, capacity),
                    "tile",
                    split_axis=0,
                    concat_axis=0,
                    tiled=True,
                )
            grad_sum = jnp.dot(
                select.T,
                got_terms.reshape(buffer_size, frame_count),
                precision=lax.Precision.HIGHEST,
            )
            current = jnp.maximum(current - grad_sum * scale_row[:, None], 0.0)
    slot_low = slot_traces.astype(jnp.bfloat16)
    data_term = lax.dot_general(
        recording, slot_low, (((1,), (1,)), ((), ())), preferred_element_type=jnp.float32
    )
    trace_term = jnp.dot(slot_traces, slot_traces.T, precision=lax.Precision.HIGHEST)
    data_sum = sum_at_owner(data_term, "frame", 0)
    trace_gram = over_copies(trace_term, "frame")
    share_rows = data_sum.shape[0]
    local_block = lax.dynamic_slice_in_dim(
        footprints, lax.axis_index("frame") * share_rows, share_rows, 0
    )
    column_step = 1.0 / (1.0 + jnp.sum(jnp.abs(trace_gram), axis=1))
    support = local_block > 0
    iterate = local_block.astype(jnp.float32)
    for sweep in range(ITER_A):
        moved = (
            iterate
            - (jnp.dot(iterate, trace_gram, precision=lax.Precision.HIGHEST) - data_sum)
            * column_step[None, :]
        )
        iterate = jnp.where(support, jnp.maximum(moved, 0.0), jnp.zeros_like(moved))
    updated = iterate.astype(jnp.bfloat16)
    updated = gathered_copies(updated, "frame", 0)
    return (current, updated)


def solution(mesh):
    in_specs = (P("tile", "frame"), P("tile", None), P("tile", None), P("tile"), P("tile", "frame"))
    out_specs = (P("tile", "frame"), P("tile", None))
    return jax.shard_map(body, mesh=mesh, in_specs=in_specs, out_specs=out_specs, check_vma=False)
```

```python
import jax
import jax.numpy as jnp
from jax import lax
from jax.experimental import pallas as pl
from jax.experimental.pallas import tpu as pltpu
from jax.sharding import PartitionSpec as P

ITER_C = 4
ITER_A = 8
RING = 8
CHIPS = 64
XS = 4
PICKS = 40
K = 128
V = 1024
MESH = pl.DeviceIdType.MESH
F32 = jnp.float32
BF16 = jnp.bfloat16
I32 = jnp.int32


def dot(a, b):
    return jnp.dot(a, b, preferred_element_type=F32)


def dot_t(a, b):
    return lax.dot_general(a, b, (((0,), (0,)), ((), ())), preferred_element_type=F32)


def split(v):
    hi = v.astype(BF16)
    return hi, (v - hi.astype(F32)).astype(BF16)


def remote(src, dst, send, recv, tile, frame):
    return pltpu.make_async_remote_copy(
        src_ref=src, dst_ref=dst, send_sem=send, recv_sem=recv, device_id=(tile, frame), device_id_type=MESH
    )


def drain(ref, sem):
    pltpu.make_async_copy(ref, ref, sem).wait()


def ring_order(i):
    half = (i + 1) // 2
    return lax.rem(RING + half * (2 * (i % 2) - 1), RING)


def pick_rows(table, row, pick):
    low, high = jnp.bitwise_and(pick, 7), pick >> 3
    out = jnp.zeros(pick.shape, F32)
    for j in range(PICKS // 8):
        got = jnp.take_along_axis(table[row + 8 * j : row + 8 * j + 8, :], low, axis=0)
        out = jnp.where(high == j, got, out)
    return out


def kernel(
    rec, foot, owner_in, pick_in, traces,
    out_traces, out_foot,
    grams, msg, got, half, part, part_in, bound_in, table, scale, s_buf, back, back_in, s_all, y_all, x_buf, q_buf, a_buf, w_buf,
    pick_s, slot_s, lane_s, rank_s, turn,
    gram_send, gram_one, gram_two, msg_send, msg_recv, core_send, core_recv, back_send, back_recv, x_send, x_recv, y_send, y_recv, here_sem,
):
    me = lax.axis_index("tile")
    x = lax.axis_index("frame")
    c = lax.rem(me, 2)
    q = me // 2
    zc, yc = q // RING, lax.rem(q, RING)
    sibling = me + 1 - 2 * c
    a = zc * (1 - c) + yc * c
    b = yc * (1 - c) + zc * c
    sa, sb = RING - (RING - 1) * c, 1 + (RING - 1) * c

    barrier = pltpu.get_barrier_semaphore()

    def greet(i, carry):
        pl.semaphore_signal(barrier, inc=1, device_id=(lax.rem(q + i, CHIPS) * 2 + c, x), device_id_type=MESH)
        return carry

    lax.fori_loop(1, CHIPS, greet, 0)
    pl.semaphore_signal(barrier, inc=1, device_id=(sibling, x), device_id_type=MESH)
    for i in range(1, XS):
        pl.semaphore_signal(barrier, inc=1, device_id=(me, lax.rem(x + i, XS)), device_id_type=MESH)

    block = foot[...]
    gram = dot_t(block, block)
    drive = dot_t(rec[...], block)
    grams[q] = gram.astype(BF16)
    bound = jnp.sum(jnp.abs(gram), axis=0, keepdims=True)
    lane = lax.broadcasted_iota(I32, (K, K), 1)
    sub = lax.broadcasted_iota(I32, (K, K), 0)
    own = owner_in[...]
    own = jnp.broadcast_to((own & 1) * CHIPS + (own >> 1), (K, K))
    own_t = jnp.transpose(own.astype(F32)).astype(I32)
    pick_t = jnp.transpose(jnp.broadcast_to(pick_in[...], (K, K)).astype(F32)).astype(I32)
    same = own == own_t
    rank_row = jnp.sum(jnp.where(same & (sub < lane), 1.0, 0.0), axis=0, keepdims=True)
    rank_col = jnp.sum(jnp.where(same & (lane < sub), 1.0, 0.0), axis=1, keepdims=True)
    code = (pick_t * K + sub + 1).astype(F32)
    here = own_t == lane
    code0 = jnp.sum(jnp.where(here & (rank_col < 0.5), code, 0.0), axis=0, keepdims=True)
    code1 = jnp.sum(jnp.where(here & (rank_col > 0.5), code, 0.0), axis=0, keepdims=True)
    slot_code = own[0:1, :].astype(F32) * 2.0 + rank_row
    by_frame = jnp.transpose(traces[0:K, :])
    low_lane = lax.broadcasted_iota(I32, (CHIPS, K), 1) < CHIPS
    rows = (
        drive[0:CHIPS],
        drive[CHIPS:K],
        jnp.where(low_lane, by_frame[0:CHIPS], pltpu.roll(by_frame[CHIPS:K], CHIPS, 1)),
        jnp.broadcast_to(code0, (CHIPS, K)),
        jnp.broadcast_to(code1, (CHIPS, K)),
        jnp.broadcast_to(slot_code, (CHIPS, K)),
        jnp.broadcast_to(bound, (CHIPS, K)),
        jnp.zeros((CHIPS, K), F32),
    )
    for j, row in enumerate(rows):
        msg[pl.ds(j, CHIPS, stride=8), :] = row
    got[pl.ds(pl.multiple_of(q * 8, 8), 8), :] = msg[pl.ds(pl.multiple_of(q * 8, 8), 8), :]

    pl.semaphore_wait(barrier, CHIPS - 1 + 1 + XS - 1)

    up = (a * sa + lax.rem(b + 1, RING) * sb) * 2 + c
    down = (a * sa + lax.rem(b + RING - 1, RING) * sb) * 2 + c

    def forward(step, i, off, want_up, want_down):
        r = ring_order(i)
        column = lax.rem(a + r, RING) * sa
        if want_up:
            p = column + lax.rem(b + RING - off, RING) * sb
            remote(grams.at[p], grams.at[p], gram_send, gram_two.at[step, 0, i], up, x).start()
        if want_down:
            p = column + lax.rem(b + off, RING) * sb
            remote(grams.at[p], grams.at[p], gram_send, gram_two.at[step, 1, i], down, x).start()

    forward(0, 0, 0, True, True)

    def first(i, carry):
        r = ring_order(i)
        peer = (lax.rem(a + RING - r, RING) * sa + b * sb) * 2 + c
        remote(grams.at[q], grams.at[q], gram_send, gram_one.at[i], peer, x).start()
        return carry

    lax.fori_loop(1, RING, first, 0)

    def tell(i, carry):
        p = lax.rem(q + i, CHIPS)
        remote(
            msg.at[pl.ds(pl.multiple_of(p * 8, 8), 8)],
            got.at[pl.ds(pl.multiple_of(q * 8, 8), 8)],
            msg_send, msg_recv, p * 2 + c, x,
        ).start()
        return carry

    lax.fori_loop(1, CHIPS, tell, 0)
    for i in range(1, XS):
        remote(rec, y_all.at[x], y_send.at[i], y_recv.at[i], me, lax.rem(x + i, XS)).start()
    y_own = pltpu.make_async_copy(rec, y_all.at[x], here_sem.at[0])
    y_own.start()

    def pass_on(i, carry):
        pltpu.make_async_copy(grams.at[0], grams.at[0], gram_one.at[i]).wait()
        forward(0, i, 0, True, True)
        return carry

    lax.fori_loop(1, RING, pass_on, 0)

    def arrived(step, side, i):
        pltpu.make_async_copy(grams.at[0], grams.at[0], gram_two.at[step, side, i]).wait()

    for step in range(1, 3):

        def hop(i, carry, step=step):
            arrived(step - 1, 0, i)
            arrived(step - 1, 1, i)
            forward(step, i, step, True, True)
            return carry

        lax.fori_loop(0, RING, hop, 0)

    def last_up(i, carry):
        arrived(2, 0, i)
        arrived(2, 1, i)
        forward(3, i, 3, True, False)
        return carry

    def last_down(i, carry):
        arrived(2, 0, i)
        arrived(2, 1, i)
        forward(3, i, 3, False, True)
        return carry

    lax.fori_loop(0, RING // 2, last_up, 0)
    lax.fori_loop(RING // 2, RING, last_down, 0)

    drain(got.at[pl.ds(0, (CHIPS - 1) * 8)], msg_recv)
    half[c] = got[pl.ds(2, CHIPS, stride=8), :]
    swap = remote(half.at[c], half.at[c], core_send.at[0], core_recv.at[0], sibling, x)
    swap.start()
    for r in range(2):
        m = got[pl.ds(3 + r, CHIPS, stride=8), :].astype(I32) - 1
        pick_s[r] = m >> 7
        slot_s[r] = m & (K - 1)
    m = got[pl.ds(5, CHIPS, stride=8), :].astype(I32)
    lane_s[...] = m >> 1
    rank_s[...] = m & 1

    def scatter(n, into):
        def eight(j, carry):
            base = pl.multiple_of(j * 8, 8)
            sums = [[jnp.zeros((8, K), F32) for _ in range(8)] for _ in range(n)]
            for r in range(2):
                for g in range(CHIPS // 8):
                    p = pick_s[r, 8 * g : 8 * g + 8, :] - base
                    vals = [turn[r, f, 8 * g : 8 * g + 8, :] for f in range(n)]
                    for k in range(8):
                        hit = p == k
                        for f in range(n):
                            sums[f][k] = sums[f][k] + jnp.where(hit, vals[f], 0.0)
            for f in range(n):
                done = [jnp.sum(sums[f][k], axis=0, keepdims=True) for k in range(8)]
                into[pl.ds(pl.multiple_of(base + f * PICKS, 8), 8), :] = jnp.concatenate(done, axis=0)
            return carry

        lax.fori_loop(0, PICKS // 8, eight, 0)

    for g in range(CHIPS // 8):
        s8 = slice(8 * g, 8 * g + 8)
        vals = got[pl.ds(64 * g + 6, 8, stride=8), :]
        for r in range(2):
            turn[r, 0, s8, :] = jnp.take_along_axis(vals, slot_s[r, s8, :], axis=1)
    scatter(1, part.at[0])
    bound_swap = remote(
        part.at[0, pl.ds(0, PICKS)], bound_in, core_send.at[1], core_recv.at[1], sibling, x
    )
    bound_swap.start()
    swap.wait()
    table[...] = jnp.transpose(jnp.concatenate([half[0], half[1]], axis=0))
    bound_swap.wait()
    scale[...] = 1.0 / (1.0 + (part[0, 0:PICKS, :] + bound_in[...]))

    def gathered(f, g):
        s8 = slice(8 * g, 8 * g + 8)
        lanes = lane_s[s8, :]
        first_rank = jnp.take_along_axis(pick_rows(table, f * CHIPS, pick_s[0, s8, :]), lanes, axis=1)
        second_rank = jnp.take_along_axis(pick_rows(table, f * CHIPS, pick_s[1, s8, :]), lanes, axis=1)
        return jnp.where(rank_s[s8, :] == 0, first_rank, second_rank)

    for i in range(4):
        def last(k, carry, i=i):
            arrived(3, i // 2, k)
            return carry
        if i == 0:
            lax.fori_loop(0, RING // 2, last, 0)
        if i == 2:
            lax.fori_loop(RING // 2, RING, last, 0)

    sub8 = lax.broadcasted_iota(I32, (8, K), 0)

    def sweep(it, carry):
        for g in range(CHIPS // 8):
            s8 = slice(8 * g, 8 * g + 8)
            h0, l0 = split(gathered(0, g))
            h1, l1 = split(gathered(1, g))
            left = jnp.concatenate([h0, l0, h1, l1], axis=0)
            g0 = -got[pl.ds(64 * g, 8, stride=8), :]
            g1 = -got[pl.ds(64 * g + 1, 8, stride=8), :]
            for j in range(8):
                m = dot(left, grams[8 * g + j])
                g0 = g0 + jnp.where(sub8 == j, m[0:8] + m[8:16], 0.0)
                g1 = g1 + jnp.where(sub8 == j, m[16:24] + m[24:32], 0.0)
            for r in range(2):
                slots = slot_s[r, s8, :]
                turn[r, 0, s8, :] = jnp.take_along_axis(g0, slots, axis=1)
                turn[r, 1, s8, :] = jnp.take_along_axis(g1, slots, axis=1)
        mine = part.at[it + 1]
        scatter(2, mine)
        trade = remote(mine, part_in.at[it], core_send.at[it + 2], core_recv.at[it + 2], sibling, x)
        trade.start()
        trade.wait()
        for f in range(2):
            total = part[it + 1, f * PICKS : (f + 1) * PICKS, :] + part_in[it, f * PICKS : (f + 1) * PICKS, :]
            rows = slice(f * CHIPS, f * CHIPS + PICKS)
            table[rows, :] = jnp.maximum(table[rows, :] - total * scale[...], 0.0)
        return carry

    lax.fori_loop(0, ITER_C, sweep, 0)

    for g in range(CHIPS // 8):
        for f in range(2):
            back[pl.ds(32 * g + f, 8, stride=4), :] = gathered(f, g)
    s_buf[...] = jnp.transpose(table[...])
    back[pl.ds(2, CHIPS, stride=4), :] = s_buf[pl.ds(pl.multiple_of(c * CHIPS, CHIPS), CHIPS), :]
    back[pl.ds(3, CHIPS, stride=4), :] = jnp.zeros((CHIPS, K), F32)

    def give(i, carry):
        p = lax.rem(q + i, CHIPS)
        remote(
            back.at[pl.ds(pl.multiple_of(p * 4, 4), 4)],
            back_in.at[pl.ds(pl.multiple_of(q * 4, 4), 4)],
            back_send, back_recv, p * 2 + c, x,
        ).start()
        return carry

    lax.fori_loop(1, CHIPS, give, 0)
    mine = pl.ds(pl.multiple_of(q * 4, 4), 4)
    own_back = pltpu.make_async_copy(back.at[mine], back_in.at[mine], here_sem.at[1])
    own_back.start()
    own_back.wait()
    drain(back_in.at[pl.ds(0, (CHIPS - 1) * 4)], back_recv)

    slot_traces = jnp.concatenate([back_in[pl.ds(0, CHIPS, stride=4), :], back_in[pl.ds(1, CHIPS, stride=4), :]], axis=0)
    hi, lo = split(slot_traces)
    s_all[x, :, 0:K] = hi
    s_all[x, :, K : 2 * K] = lo
    sends = []
    for i in range(1, XS):
        sends.append(remote(s_all.at[x], s_all.at[x], x_send.at[i], x_recv.at[i], me, lax.rem(x + i, XS)))
    for s in sends:
        s.start()

    held = back_in[pl.ds(2, CHIPS, stride=4), :]
    both = jnp.transpose(jnp.concatenate([held, pltpu.roll(held, CHIPS, 1)], axis=0))
    out_traces[0:PICKS, :] = both[0:PICKS]
    out_traces[PICKS:, :] = jnp.maximum(traces[PICKS:, :], 0.0)

    y_own.wait()
    for i in range(1, XS):
        remote(rec, y_all.at[x], y_send.at[i], y_recv.at[i], me, lax.rem(x + i, XS)).wait()
    for s in sends:
        s.wait()

    p_hi = jnp.zeros((K, K), F32)
    p_mix = jnp.zeros((K, K), F32)
    for i in range(XS):
        m = dot_t(s_all[i, :, 0:K], s_all[i])
        p_hi = p_hi + m[:, 0:K]
        p_mix = p_mix + m[:, K : 2 * K]
    p = p_hi + (p_mix + jnp.transpose(p_mix))
    step_row = 1.0 / (1.0 + jnp.sum(jnp.abs(p), axis=0, keepdims=True))
    w_hi, w_lo = split(p * step_row)
    w_buf[0:K, 0:K] = w_hi
    w_buf[0:K, K : 2 * K] = w_lo
    w_buf[K : 2 * K, 0:K] = w_hi
    w_buf[K : 2 * K, K : 2 * K] = jnp.zeros((K, K), BF16)
    for n in range(V // K):
        rows = slice(n * K, (n + 1) * K)
        total = dot(y_all[0, rows, :], s_all[0, :, 0:K])
        for i in range(1, XS):
            total = total + dot(y_all[i, rows, :], s_all[i, :, 0:K])
        start = foot[rows, :].astype(F32)
        q_buf[rows, :] = jnp.where(start > 0.0, total * step_row, -jnp.inf)
        x_buf[rows, :] = start

    def refine(n, carry):
        for k in range(V // K):
            rows = slice(k * K, (k + 1) * K)
            cur = x_buf[rows, :]
            hi, lo = split(cur)
            m = dot(jnp.concatenate([hi, lo], axis=1), w_buf[...])
            moved = cur - (m[:, 0:K] + m[:, K : 2 * K]) + q_buf[rows, :]
            x_buf[rows, :] = jnp.maximum(moved, 0.0)
        return carry

    lax.fori_loop(0, ITER_A, refine, 0)
    out_foot[...] = x_buf[...].astype(BF16)

    drain(grams.at[pl.ds(0, CHIPS - 1)], gram_send)
    drain(msg.at[pl.ds(0, (CHIPS - 1) * 8)], msg_send)
    drain(back.at[pl.ds(0, (CHIPS - 1) * 4)], back_send)


def body(recording, footprints, slot_owner, slot_pick, traces):
    vmem = pl.BlockSpec(memory_space=pltpu.VMEM)
    dma = pltpu.SemaphoreType.DMA
    return pl.pallas_call(
        kernel,
        out_shape=(
            jax.ShapeDtypeStruct(traces.shape, F32),
            jax.ShapeDtypeStruct(footprints.shape, BF16),
        ),
        in_specs=[vmem] * 5,
        out_specs=(vmem, vmem),
        scratch_shapes=[
            pltpu.VMEM((CHIPS, K, K), BF16),
            pltpu.VMEM((CHIPS * 8, K), F32),
            pltpu.VMEM((CHIPS * 8, K), F32),
            pltpu.VMEM((2, CHIPS, K), F32),
            pltpu.VMEM((ITER_C + 1, 2 * PICKS, K), F32),
            pltpu.VMEM((ITER_C, 2 * PICKS, K), F32),
            pltpu.VMEM((PICKS, K), F32),
            pltpu.VMEM((K, K), F32),
            pltpu.VMEM((PICKS, K), F32),
            pltpu.VMEM((K, K), F32),
            pltpu.VMEM((CHIPS * 4, K), F32),
            pltpu.VMEM((CHIPS * 4, K), F32),
            pltpu.VMEM((XS, K, 2 * K), BF16),
            pltpu.VMEM((XS, V, K), BF16),
            pltpu.VMEM((V, K), F32),
            pltpu.VMEM((V, K), F32),
            pltpu.VMEM((8, K), F32),
            pltpu.VMEM((2 * K, 2 * K), BF16),
            pltpu.VMEM((2, CHIPS, K), I32),
            pltpu.VMEM((2, CHIPS, K), I32),
            pltpu.VMEM((CHIPS, K), I32),
            pltpu.VMEM((CHIPS, K), I32),
            pltpu.VMEM((2, 2, CHIPS, K), F32),
            dma,
            dma((RING,)),
            dma((4, 2, RING)),
            dma,
            dma,
            dma((ITER_C + 2,)),
            dma((ITER_C + 2,)),
            dma,
            dma,
            dma((XS,)),
            dma((XS,)),
            dma((XS,)),
            dma((XS,)),
            dma((2,)),
        ],
        compiler_params=pltpu.CompilerParams(
            collective_id=0, has_side_effects=True, vmem_limit_bytes=40 << 20
        ),
    )(recording, footprints, slot_owner.reshape(1, K), slot_pick.reshape(1, K), traces)


def solution(mesh):
    in_specs = (P("tile", "frame"), P("tile", None), P("tile", None), P("tile"), P("tile", "frame"))
    out_specs = (P("tile", "frame"), P("tile", None))
    return jax.shard_map(body, mesh=mesh, in_specs=in_specs, out_specs=out_specs, check_vma=False)
```

```python
import jax
import jax.numpy as jnp
from jax import lax
from jax.experimental import pallas as pl
from jax.experimental.pallas import tpu as pltpu
from jax.sharding import PartitionSpec as P

ITER_C = 4
ITER_A = 8
LATE = 8
TELL = 7
RING = 8
CHIPS = 64
XS = 4
PICKS = 40
K = 128
V = 1024
MESH = pl.DeviceIdType.MESH
F32 = jnp.float32
BF16 = jnp.bfloat16
I32 = jnp.int32


def dot(a, b):
    return jnp.dot(a, b, preferred_element_type=F32)


def dot_t(a, b):
    return lax.dot_general(a, b, (((0,), (0,)), ((), ())), preferred_element_type=F32)


def split(v):
    hi = v.astype(BF16)
    return hi, (v - hi.astype(F32)).astype(BF16)


def remote(src, dst, send, recv, tile, frame):
    return pltpu.make_async_remote_copy(
        src_ref=src, dst_ref=dst, send_sem=send, recv_sem=recv, device_id=(tile, frame), device_id_type=MESH
    )


def drain(ref, sem):
    pltpu.make_async_copy(ref, ref, sem).wait()


def ring_order(i):
    half = (i + 1) // 2
    return lax.rem(RING + half * (2 * (i % 2) - 1), RING)


def pick_rows(table, row, pick):
    low, high = jnp.bitwise_and(pick, 7), pick >> 3
    out = jnp.zeros(pick.shape, F32)
    for j in range(PICKS // 8):
        got = jnp.take_along_axis(table[row + 8 * j : row + 8 * j + 8, :], low, axis=0)
        out = jnp.where(high == j, got, out)
    return out


def kernel(
    rec_hbm, foot_hbm, owner_hbm, pick_hbm, traces_hbm,
    out_traces, out_foot,
    rec, foot, owner_in, pick_in, traces,
    grams, msg, got, half, part, part_in, bound_in, table, scale, s_buf, back, back_in, s_all, y_all, x_buf, q_buf, w_buf,
    pick_s, slot_s, lane_s, rank_s, turn,
    gram_send, gram_one, gram_two, msg_send, msg_recv, core_send, core_recv, back_send, back_recv, x_send, x_recv, y_send, y_recv, here_sem, load_sem, ready,
):
    me = lax.axis_index("tile")
    x = lax.axis_index("frame")
    c = lax.rem(me, 2)
    q = me // 2
    zc, yc = q // RING, lax.rem(q, RING)
    sibling = me + 1 - 2 * c
    a = zc * (1 - c) + yc * c
    b = yc * (1 - c) + zc * c
    sa, sb = RING - (RING - 1) * c, 1 + (RING - 1) * c

    def ring_a(r):
        return (lax.rem(a + r, RING) * sa + b * sb) * 2 + c

    def ring_b(r):
        return (a * sa + lax.rem(b + r, RING) * sb) * 2 + c

    loads = [
        pltpu.make_async_copy(src, dst, load_sem.at[n])
        for n, (src, dst) in enumerate(
            ((foot_hbm, foot), (rec_hbm, rec), (owner_hbm, owner_in), (pick_hbm, pick_in), (traces_hbm, traces))
        )
    ]
    for load in loads:
        load.start()
    barrier = pltpu.get_barrier_semaphore()
    for r in (4, 3, 5, 2, 6, 1, 7):
        pl.semaphore_signal(barrier, inc=1, device_id=(ring_a(r), x), device_id_type=MESH)
        pl.semaphore_signal(barrier, inc=1, device_id=(ring_b(r), x), device_id_type=MESH)
    for i in range(1, XS):
        pl.semaphore_signal(barrier, inc=1, device_id=(me, lax.rem(x + i, XS)), device_id_type=MESH)
    pl.semaphore_signal(barrier, inc=1, device_id=(sibling, x), device_id_type=MESH)
    for load in loads:
        load.wait()

    block = foot[...]
    gram = dot_t(block, block)
    drive = dot_t(rec[...], block)
    grams[q] = gram.astype(BF16)
    bound = jnp.sum(jnp.abs(gram), axis=0, keepdims=True)
    lane = lax.broadcasted_iota(I32, (K, K), 1)
    sub = lax.broadcasted_iota(I32, (K, K), 0)
    rest = jnp.sum(jnp.where(lane == sub, gram - gram.astype(BF16).astype(F32), 0.0), axis=0, keepdims=True)
    own = owner_in[...]
    own = jnp.broadcast_to((own & 1) * CHIPS + (own >> 1), (K, K))
    own_t = jnp.transpose(own.astype(F32)).astype(I32)
    pick_t = jnp.transpose(jnp.broadcast_to(pick_in[...], (K, K)).astype(F32)).astype(I32)
    same = own == own_t
    rank_row = jnp.sum(jnp.where(same & (sub < lane), 1.0, 0.0), axis=0, keepdims=True)
    rank_col = jnp.sum(jnp.where(same & (lane < sub), 1.0, 0.0), axis=1, keepdims=True)
    code = (pick_t * K + sub + 1).astype(F32)
    here = own_t == lane
    code0 = jnp.sum(jnp.where(here & (rank_col < 0.5), code, 0.0), axis=0, keepdims=True)
    code1 = jnp.sum(jnp.where(here & (rank_col > 0.5), code, 0.0), axis=0, keepdims=True)
    slot_code = own[0:1, :].astype(F32) * 2.0 + rank_row
    by_frame = jnp.transpose(traces[0:K, :])
    low_lane = lax.broadcasted_iota(I32, (CHIPS, K), 1) < CHIPS
    rows = (
        drive[0:CHIPS],
        drive[CHIPS:K],
        jnp.where(low_lane, by_frame[0:CHIPS], pltpu.roll(by_frame[CHIPS:K], CHIPS, 1)),
        jnp.broadcast_to(code0, (CHIPS, K)),
        jnp.broadcast_to(code1, (CHIPS, K)),
        jnp.broadcast_to(slot_code, (CHIPS, K)),
        jnp.broadcast_to(bound, (CHIPS, K)),
        jnp.broadcast_to(rest, (CHIPS, K)),
    )
    for j, row in enumerate(rows):
        msg[pl.ds(j, CHIPS, stride=8), :] = row
    got[pl.ds(pl.multiple_of(q * 8, 8), 8), :] = msg[pl.ds(pl.multiple_of(q * 8, 8), 8), :]

    pl.semaphore_wait(barrier, 2 * (RING - 1) + XS)
    for r in (4, 3, 5, 2, 6, 1, 7):
        pl.semaphore_signal(ready, inc=1, device_id=(ring_b(r), x), device_id_type=MESH)

    def forward(i, off, hop, up=True, down=True):
        column = lax.rem(a + ring_order(i), RING) * sa
        if up:
            p = column + lax.rem(b + RING - off, RING) * sb
            remote(grams.at[p], grams.at[p], gram_send, gram_two.at[off + hop - 1, 0, i], ring_b(hop), x).start()
        if down:
            p = column + lax.rem(b + off, RING) * sb
            remote(grams.at[p], grams.at[p], gram_send, gram_two.at[off + hop - 1, 1, i], ring_b(RING - hop), x).start()

    def arrived(off, i, up=True, down=True):
        if up:
            pltpu.make_async_copy(grams.at[0], grams.at[0], gram_two.at[off - 1, 0, i]).wait()
        if down:
            pltpu.make_async_copy(grams.at[0], grams.at[0], gram_two.at[off - 1, 1, i]).wait()

    def tell(n):
        rz, ry = ring_order(RING - 1 - n // RING), ring_order(RING - 1 - lax.rem(n, RING))
        p = lax.rem(zc + rz, RING) * RING + lax.rem(yc + ry, RING)
        remote(
            msg.at[pl.ds(pl.multiple_of(p * 8, 8), 8)],
            got.at[pl.ds(pl.multiple_of(q * 8, 8), 8)],
            msg_send, msg_recv, p * 2 + c, x,
        ).start()

    def loop(start, stop, step):
        def run(i, carry):
            step(i)
            return carry

        lax.fori_loop(start, stop, run, 0)

    forward(0, 0, 1)
    loop(1, RING, lambda i: remote(
        grams.at[q], grams.at[q], gram_send, gram_one.at[RING - i], ring_a(RING - ring_order(RING - i)), x
    ).start())
    for i in range(1, XS):
        remote(rec, y_all.at[x], y_send.at[i], y_recv.at[i], me, lax.rem(x + i, XS)).start()
    y_own = pltpu.make_async_copy(rec, y_all.at[x], here_sem.at[0])
    y_own.start()

    def pass_on(i):
        pltpu.make_async_copy(grams.at[0], grams.at[0], gram_one.at[i]).wait()
        forward(i, 0, 1)

    def some(n):
        loop(n * TELL, (n + 1) * TELL, tell)

    loop(1, LATE, pass_on)
    pl.semaphore_wait(ready, RING - 1)

    def pass_late(i):
        pass_on(i)
        forward(i, 0, 2)
        some(i - LATE)

    loop(LATE, RING, pass_late)

    def second(i):
        arrived(1, i)
        forward(i, 1, 1)
        some(RING - LATE + i)

    loop(0, LATE, second)
    loop(RING * TELL, CHIPS - 1, tell)

    def third_up(i):
        arrived(2, i)
        forward(i, 2, 1)
        forward(i, 2, 2, down=False)

    def third_down(i):
        arrived(2, i)
        forward(i, 2, 1)
        forward(i, 2, 2, up=False)

    loop(0, RING // 2, third_up)
    loop(RING // 2, RING, third_down)

    drain(got.at[pl.ds(0, (CHIPS - 1) * 8)], msg_recv)
    half[c] = got[pl.ds(2, CHIPS, stride=8), :]
    swap = remote(half.at[c], half.at[c], core_send.at[0], core_recv.at[0], sibling, x)
    swap.start()
    for r in range(2):
        m = got[pl.ds(3 + r, CHIPS, stride=8), :].astype(I32) - 1
        pick_s[r] = m >> 7
        slot_s[r] = m & (K - 1)
    m = got[pl.ds(5, CHIPS, stride=8), :].astype(I32)
    lane_s[...] = m >> 1
    rank_s[...] = m & 1

    def scatter(n, into):
        def eight(j, carry):
            base = pl.multiple_of(j * 8, 8)
            sums = [[jnp.zeros((8, K), F32) for _ in range(8)] for _ in range(n)]
            for r in range(2):
                for g in range(CHIPS // 8):
                    p = pick_s[r, 8 * g : 8 * g + 8, :] - base
                    vals = [turn[r, f, 8 * g : 8 * g + 8, :] for f in range(n)]
                    for k in range(8):
                        hit = p == k
                        for f in range(n):
                            sums[f][k] = sums[f][k] + jnp.where(hit, vals[f], 0.0)
            for f in range(n):
                done = [jnp.sum(sums[f][k], axis=0, keepdims=True) for k in range(8)]
                into[pl.ds(pl.multiple_of(base + f * PICKS, 8), 8), :] = jnp.concatenate(done, axis=0)
            return carry

        lax.fori_loop(0, PICKS // 8, eight, 0)

    for g in range(CHIPS // 8):
        s8 = slice(8 * g, 8 * g + 8)
        vals = got[pl.ds(64 * g + 6, 8, stride=8), :]
        for r in range(2):
            turn[r, 0, s8, :] = jnp.take_along_axis(vals, slot_s[r, s8, :], axis=1)
    scatter(1, part.at[0])
    bound_swap = remote(
        part.at[0, pl.ds(0, PICKS)], bound_in, core_send.at[1], core_recv.at[1], sibling, x
    )
    bound_swap.start()
    swap.wait()
    table[...] = jnp.transpose(jnp.concatenate([half[0], half[1]], axis=0))
    bound_swap.wait()
    scale[...] = 1.0 / (1.0 + (part[0, 0:PICKS, :] + bound_in[...]))

    def gathered(f, g):
        s8 = slice(8 * g, 8 * g + 8)
        lanes = lane_s[s8, :]
        first_rank = jnp.take_along_axis(pick_rows(table, f * CHIPS, pick_s[0, s8, :]), lanes, axis=1)
        second_rank = jnp.take_along_axis(pick_rows(table, f * CHIPS, pick_s[1, s8, :]), lanes, axis=1)
        return jnp.where(rank_s[s8, :] == 0, first_rank, second_rank)

    loop(LATE, RING, lambda i: arrived(1, i))
    loop(0, RING, lambda i: arrived(3, i))
    loop(0, RING // 2, lambda i: arrived(4, i, down=False))
    loop(RING // 2, RING, lambda i: arrived(4, i, up=False))

    sub8 = lax.broadcasted_iota(I32, (8, K), 0)

    def sweep(it, carry):
        for g in range(CHIPS // 8):
            s8 = slice(8 * g, 8 * g + 8)
            s0, s1 = gathered(0, g), gathered(1, g)
            h0, l0 = split(s0)
            h1, l1 = split(s1)
            extra = got[pl.ds(64 * g + 7, 8, stride=8), :]
            left = jnp.concatenate([h0, l0, h1, l1], axis=0)
            g0 = extra * s0 - got[pl.ds(64 * g, 8, stride=8), :]
            g1 = extra * s1 - got[pl.ds(64 * g + 1, 8, stride=8), :]
            for j in range(8):
                m = dot(left, grams[8 * g + j])
                g0 = g0 + jnp.where(sub8 == j, m[0:8] + m[8:16], 0.0)
                g1 = g1 + jnp.where(sub8 == j, m[16:24] + m[24:32], 0.0)
            for r in range(2):
                slots = slot_s[r, s8, :]
                turn[r, 0, s8, :] = jnp.take_along_axis(g0, slots, axis=1)
                turn[r, 1, s8, :] = jnp.take_along_axis(g1, slots, axis=1)
        mine = part.at[it + 1]
        scatter(2, mine)
        trade = remote(mine, part_in.at[it], core_send.at[it + 2], core_recv.at[it + 2], sibling, x)
        trade.start()
        trade.wait()
        for f in range(2):
            total = part[it + 1, f * PICKS : (f + 1) * PICKS, :] + part_in[it, f * PICKS : (f + 1) * PICKS, :]
            rows = slice(f * CHIPS, f * CHIPS + PICKS)
            table[rows, :] = jnp.maximum(table[rows, :] - total * scale[...], 0.0)
        return carry

    lax.fori_loop(0, ITER_C, sweep, 0)

    for g in range(CHIPS // 8):
        for f in range(2):
            back[pl.ds(32 * g + f, 8, stride=4), :] = gathered(f, g)
    s_buf[...] = jnp.transpose(table[...])
    back[pl.ds(2, CHIPS, stride=4), :] = s_buf[pl.ds(pl.multiple_of(c * CHIPS, CHIPS), CHIPS), :]
    back[pl.ds(3, CHIPS, stride=4), :] = jnp.zeros((CHIPS, K), F32)

    away = [(rz, ry) for rz in range(RING) for ry in range(RING) if rz or ry]
    for rz, ry in sorted(away, key=lambda r: -min(r[0], RING - r[0]) - min(r[1], RING - r[1])):
        p = lax.rem(zc + rz, RING) * RING + lax.rem(yc + ry, RING)
        remote(
            back.at[pl.ds(pl.multiple_of(p * 4, 4), 4)],
            back_in.at[pl.ds(pl.multiple_of(q * 4, 4), 4)],
            back_send, back_recv, p * 2 + c, x,
        ).start()
    mine = pl.ds(pl.multiple_of(q * 4, 4), 4)
    own_back = pltpu.make_async_copy(back.at[mine], back_in.at[mine], here_sem.at[1])
    own_back.start()
    own_back.wait()
    drain(back_in.at[pl.ds(0, (CHIPS - 1) * 4)], back_recv)

    slot_traces = jnp.concatenate([back_in[pl.ds(0, CHIPS, stride=4), :], back_in[pl.ds(1, CHIPS, stride=4), :]], axis=0)
    hi, lo = split(slot_traces)
    s_all[x, :, 0:K] = hi
    s_all[x, :, K : 2 * K] = lo
    sends = []
    for i in range(1, XS):
        sends.append(remote(s_all.at[x], s_all.at[x], x_send.at[i], x_recv.at[i], me, lax.rem(x + i, XS)))
    for s in sends:
        s.start()

    held = back_in[pl.ds(2, CHIPS, stride=4), :]
    both = jnp.transpose(jnp.concatenate([held, pltpu.roll(held, CHIPS, 1)], axis=0))
    out_traces[0:PICKS, :] = both[0:PICKS]
    out_traces[PICKS:, :] = jnp.maximum(traces[PICKS:, :], 0.0)

    y_own.wait()
    for i in range(1, XS):
        remote(rec, y_all.at[x], y_send.at[i], y_recv.at[i], me, lax.rem(x + i, XS)).wait()
    for s in sends:
        s.wait()

    p_hi = jnp.zeros((K, K), F32)
    p_mix = jnp.zeros((K, K), F32)
    for i in range(XS):
        m = dot_t(s_all[i, :, 0:K], s_all[i])
        p_hi = p_hi + m[:, 0:K]
        p_mix = p_mix + m[:, K : 2 * K]
    p = p_hi + (p_mix + jnp.transpose(p_mix))
    step_row = 1.0 / (1.0 + jnp.sum(jnp.abs(p), axis=0, keepdims=True))
    w_hi, w_lo = split(p * step_row)
    w_buf[0:K, 0:K] = w_hi
    w_buf[0:K, K : 2 * K] = w_lo
    w_buf[K : 2 * K, 0:K] = w_hi
    w_buf[K : 2 * K, K : 2 * K] = jnp.zeros((K, K), BF16)
    for n in range(V // K):
        rows = slice(n * K, (n + 1) * K)
        total = dot(y_all[0, rows, :], s_all[0, :, 0:K])
        for i in range(1, XS):
            total = total + dot(y_all[i, rows, :], s_all[i, :, 0:K])
        start = foot[rows, :].astype(F32)
        q_buf[rows, :] = jnp.where(start > 0.0, total * step_row, -jnp.inf)
        x_buf[rows, :] = start

    def refine(n, carry):
        for k in range(V // K):
            rows = slice(k * K, (k + 1) * K)
            cur = x_buf[rows, :]
            hi, lo = split(cur)
            m = dot(jnp.concatenate([hi, lo], axis=1), w_buf[...])
            moved = cur - (m[:, 0:K] + m[:, K : 2 * K]) + q_buf[rows, :]
            x_buf[rows, :] = jnp.maximum(moved, 0.0)
        return carry

    lax.fori_loop(0, ITER_A, refine, 0)
    out_foot[...] = x_buf[...].astype(BF16)

    drain(grams.at[pl.ds(0, CHIPS - 1)], gram_send)
    drain(msg.at[pl.ds(0, (CHIPS - 1) * 8)], msg_send)
    drain(back.at[pl.ds(0, (CHIPS - 1) * 4)], back_send)


def body(recording, footprints, slot_owner, slot_pick, traces):
    vmem = pl.BlockSpec(memory_space=pltpu.VMEM)
    dma = pltpu.SemaphoreType.DMA
    return pl.pallas_call(
        kernel,
        out_shape=(
            jax.ShapeDtypeStruct(traces.shape, F32),
            jax.ShapeDtypeStruct(footprints.shape, BF16),
        ),
        in_specs=[pl.BlockSpec(memory_space=pltpu.HBM)] * 5,
        out_specs=(vmem, vmem),
        scratch_shapes=[
            pltpu.VMEM((V, K), BF16),
            pltpu.VMEM((V, K), BF16),
            pltpu.VMEM((1, K), I32),
            pltpu.VMEM((1, K), I32),
            pltpu.VMEM(traces.shape, F32),
            pltpu.VMEM((CHIPS, K, K), BF16),
            pltpu.VMEM((CHIPS * 8, K), F32),
            pltpu.VMEM((CHIPS * 8, K), F32),
            pltpu.VMEM((2, CHIPS, K), F32),
            pltpu.VMEM((ITER_C + 1, 2 * PICKS, K), F32),
            pltpu.VMEM((ITER_C, 2 * PICKS, K), F32),
            pltpu.VMEM((PICKS, K), F32),
            pltpu.VMEM((K, K), F32),
            pltpu.VMEM((PICKS, K), F32),
            pltpu.VMEM((K, K), F32),
            pltpu.VMEM((CHIPS * 4, K), F32),
            pltpu.VMEM((CHIPS * 4, K), F32),
            pltpu.VMEM((XS, K, 2 * K), BF16),
            pltpu.VMEM((XS, V, K), BF16),
            pltpu.VMEM((V, K), F32),
            pltpu.VMEM((V, K), F32),
            pltpu.VMEM((2 * K, 2 * K), BF16),
            pltpu.VMEM((2, CHIPS, K), I32),
            pltpu.VMEM((2, CHIPS, K), I32),
            pltpu.VMEM((CHIPS, K), I32),
            pltpu.VMEM((CHIPS, K), I32),
            pltpu.VMEM((2, 2, CHIPS, K), F32),
            dma,
            dma((RING,)),
            dma((4, 2, RING)),
            dma,
            dma,
            dma((ITER_C + 2,)),
            dma((ITER_C + 2,)),
            dma,
            dma,
            dma((XS,)),
            dma((XS,)),
            dma((XS,)),
            dma((XS,)),
            dma((2,)),
            dma((5,)),
            pltpu.SemaphoreType.REGULAR,
        ],
        compiler_params=pltpu.CompilerParams(
            collective_id=0, has_side_effects=True, vmem_limit_bytes=40 << 20
        ),
    )(recording, footprints, slot_owner.reshape(1, K), slot_pick.reshape(1, K), traces)


def solution(mesh):
    in_specs = (P("tile", "frame"), P("tile", None), P("tile", None), P("tile"), P("tile", "frame"))
    out_specs = (P("tile", "frame"), P("tile", None))
    return jax.shard_map(body, mesh=mesh, in_specs=in_specs, out_specs=out_specs, check_vma=False)
```

```python
import jax
import jax.numpy as jnp
from jax import lax
from jax.experimental import pallas as pl
from jax.experimental.pallas import tpu as pltpu
from jax.sharding import PartitionSpec as P

ITER_C = 4
ITER_A = 8
LATE = 8
TELL = 7
SENT = 7
ROWS = 256
RING = 8
CHIPS = 64
XS = 4
PICKS = 40
K = 128
V = 1024
MESH = pl.DeviceIdType.MESH
F32 = jnp.float32
BF16 = jnp.bfloat16
I32 = jnp.int32


def dot(a, b):
    return jnp.dot(a, b, preferred_element_type=F32)


def dot_t(a, b):
    return lax.dot_general(a, b, (((0,), (0,)), ((), ())), preferred_element_type=F32)


def split(v):
    hi = v.astype(BF16)
    return hi, (v - hi.astype(F32)).astype(BF16)


def remote(src, dst, send, recv, tile, frame):
    return pltpu.make_async_remote_copy(
        src_ref=src, dst_ref=dst, send_sem=send, recv_sem=recv, device_id=(tile, frame), device_id_type=MESH
    )


def drain(ref, sem):
    pltpu.make_async_copy(ref, ref, sem).wait()


def ring_order(i):
    half = (i + 1) // 2
    return lax.rem(RING + half * (2 * (i % 2) - 1), RING)


def pick_rows(table, row, pick):
    low, high = jnp.bitwise_and(pick, 7), pick >> 3
    out = jnp.zeros(pick.shape, F32)
    for j in range(PICKS // 8):
        got = jnp.take_along_axis(table[row + 8 * j : row + 8 * j + 8, :], low, axis=0)
        out = jnp.where(high == j, got, out)
    return out


def kernel(
    rec_hbm, foot_hbm, owner_hbm, pick_hbm, traces_hbm,
    out_traces, out_foot,
    rec, foot, owner_in, pick_in, traces,
    grams, packed, msg, got, half, part, part_in, bound_in, table, scale, s_buf, back, back_in, s_all, y_all, x_buf, q_buf, w_buf,
    pick_s, slot_s, lane_s, rank_s, turn,
    gram_send, gram_one, gram_two, msg_send, msg_recv, core_send, core_recv, back_send, back_recv, x_send, x_recv, y_send, y_recv, here_sem, load_sem, ready,
):
    me = lax.axis_index("tile")
    x = lax.axis_index("frame")
    c = lax.rem(me, 2)
    q = me // 2
    zc, yc = q // RING, lax.rem(q, RING)
    sibling = me + 1 - 2 * c
    a = zc * (1 - c) + yc * c
    b = yc * (1 - c) + zc * c
    sa, sb = RING - (RING - 1) * c, 1 + (RING - 1) * c

    def ring_a(r):
        return (lax.rem(a + r, RING) * sa + b * sb) * 2 + c

    def ring_b(r):
        return (a * sa + lax.rem(b + r, RING) * sb) * 2 + c

    loads = [
        pltpu.make_async_copy(src, dst, load_sem.at[n])
        for n, (src, dst) in enumerate(
            ((foot_hbm, foot), (rec_hbm, rec), (owner_hbm, owner_in), (pick_hbm, pick_in), (traces_hbm, traces))
        )
    ]
    for load in loads:
        load.start()
    barrier = pltpu.get_barrier_semaphore()
    for r in (4, 3, 5, 2, 6, 1, 7):
        pl.semaphore_signal(barrier, inc=1, device_id=(ring_a(r), x), device_id_type=MESH)
        pl.semaphore_signal(barrier, inc=1, device_id=(ring_b(r), x), device_id_type=MESH)
    for i in range(1, XS):
        pl.semaphore_signal(barrier, inc=1, device_id=(me, lax.rem(x + i, XS)), device_id_type=MESH)
    pl.semaphore_signal(barrier, inc=1, device_id=(sibling, x), device_id_type=MESH)
    for load in loads:
        load.wait()

    block = foot[...]
    gram = dot_t(block, block)
    drive = dot_t(rec[...], block)
    grams[q] = gram.astype(BF16)
    right = lax.broadcasted_iota(I32, (K // 4, K), 1) >= K // 2
    fold = jnp.where(right, gram[K // 2 : 3 * K // 4], pltpu.roll(gram[3 * K // 4 :], K // 2, 1))
    packed[q, 0 : K // 2] = gram[0 : K // 2].astype(BF16)
    packed[q, K // 2 :] = fold.astype(BF16)
    bound = jnp.sum(jnp.abs(gram), axis=0, keepdims=True)
    lane = lax.broadcasted_iota(I32, (K, K), 1)
    sub = lax.broadcasted_iota(I32, (K, K), 0)
    rest = jnp.sum(jnp.where(lane == sub, gram - gram.astype(BF16).astype(F32), 0.0), axis=0, keepdims=True)
    own = owner_in[...]
    own = jnp.broadcast_to((own & 1) * CHIPS + (own >> 1), (K, K))
    own_t = jnp.transpose(own.astype(F32)).astype(I32)
    same = own == own_t
    rank_col = jnp.sum(jnp.where(same & (lane < sub), 1.0, 0.0), axis=1, keepdims=True)
    place = (sub + 1).astype(F32) * jnp.where(rank_col < 0.5, 1.0, 2.0 * K)
    slots_of = jnp.sum(jnp.where(own_t == lane, place, 0.0), axis=0, keepdims=True)
    slot_row = (own[0:1, :] * CHIPS + pick_in[...]).astype(F32)
    by_frame = jnp.transpose(traces[0:K, :])
    low_lane = lax.broadcasted_iota(I32, (CHIPS, K), 1) < CHIPS
    rows = (
        drive[0:CHIPS],
        drive[CHIPS:K],
        jnp.where(low_lane, by_frame[0:CHIPS], pltpu.roll(by_frame[CHIPS:K], CHIPS, 1)),
        jnp.broadcast_to(slots_of, (CHIPS, K)),
        jnp.broadcast_to(slot_row, (CHIPS, K)),
        jnp.broadcast_to(bound, (CHIPS, K)),
        jnp.broadcast_to(rest, (CHIPS, K)),
    )
    for j, row in enumerate(rows):
        msg[pl.ds(j, CHIPS, stride=8), :] = row
    for j, row in enumerate(rows):
        got[pl.ds(q * 8 + j, 1), :] = msg[pl.ds(q * 8 + j, 1), :]

    pl.semaphore_wait(barrier, 2 * (RING - 1) + XS)
    for r in (4, 3, 5, 2, 6, 1, 7):
        pl.semaphore_signal(ready, inc=1, device_id=(ring_b(r), x), device_id_type=MESH)

    def forward(i, off, hop, up=True, down=True):
        column = lax.rem(a + ring_order(i), RING) * sa
        if up:
            p = column + lax.rem(b + RING - off, RING) * sb
            remote(packed.at[p], packed.at[p], gram_send, gram_two.at[off + hop - 1, 0, i], ring_b(hop), x).start()
        if down:
            p = column + lax.rem(b + off, RING) * sb
            remote(packed.at[p], packed.at[p], gram_send, gram_two.at[off + hop - 1, 1, i], ring_b(RING - hop), x).start()

    def unfold(p):
        high = packed[p, 0 : K // 2]
        fold = packed[p, K // 2 :]
        grams[p, 0 : K // 2] = high
        grams[p, K // 2 : 3 * K // 4] = fold
        grams[p, 3 * K // 4 :] = pltpu.roll(fold.astype(F32), K // 2, 1).astype(BF16)
        grams[p, K // 2 :, 0 : K // 2] = jnp.transpose(high.astype(F32))[K // 2 :].astype(BF16)

    def unfolded(i, off, up=True, down=True):
        column = lax.rem(a + ring_order(i), RING) * sa
        if up:
            unfold(column + lax.rem(b + RING - off, RING) * sb)
        if down:
            unfold(column + lax.rem(b + off, RING) * sb)

    def arrived(off, i, up=True, down=True):
        if up:
            pltpu.make_async_copy(packed.at[0], packed.at[0], gram_two.at[off - 1, 0, i]).wait()
        if down:
            pltpu.make_async_copy(packed.at[0], packed.at[0], gram_two.at[off - 1, 1, i]).wait()

    def tell(n):
        rz, ry = ring_order(RING - 1 - n // RING), ring_order(RING - 1 - lax.rem(n, RING))
        p = lax.rem(zc + rz, RING) * RING + lax.rem(yc + ry, RING)
        remote(
            msg.at[pl.ds(pl.multiple_of(p * 8, 8), SENT)],
            got.at[pl.ds(pl.multiple_of(q * 8, 8), SENT)],
            msg_send, msg_recv, p * 2 + c, x,
        ).start()

    def loop(start, stop, step):
        def run(i, carry):
            step(i)
            return carry

        lax.fori_loop(start, stop, run, 0)

    forward(0, 0, 1)
    loop(1, RING, lambda i: remote(
        packed.at[q], packed.at[q], gram_send, gram_one.at[RING - i], ring_a(RING - ring_order(RING - i)), x
    ).start())
    for i in range(1, XS):
        remote(rec, y_all.at[x], y_send.at[i], y_recv.at[i], me, lax.rem(x + i, XS)).start()
    y_own = pltpu.make_async_copy(rec, y_all.at[x], here_sem.at[0])
    y_own.start()

    def pass_on(i):
        pltpu.make_async_copy(packed.at[0], packed.at[0], gram_one.at[i]).wait()
        forward(i, 0, 1)
        unfolded(i, 0, down=False)

    def some(n):
        loop(n * TELL, (n + 1) * TELL, tell)

    loop(1, LATE, pass_on)
    pl.semaphore_wait(ready, RING - 1)

    def pass_late(i):
        pass_on(i)
        forward(i, 0, 2)
        some(i - LATE)

    loop(LATE, RING, pass_late)

    def second(i):
        arrived(1, i)
        forward(i, 1, 1)
        some(RING - LATE + i)
        unfolded(i, 1)

    loop(0, LATE, second)
    loop(RING * TELL, CHIPS - 1, tell)

    def third_up(i):
        arrived(2, i)
        forward(i, 2, 1)
        forward(i, 2, 2, down=False)
        unfolded(i, 2)

    def third_down(i):
        arrived(2, i)
        forward(i, 2, 1)
        forward(i, 2, 2, up=False)
        unfolded(i, 2)

    loop(0, RING // 2, third_up)
    loop(RING // 2, RING, third_down)

    drain(got.at[pl.ds(0, (CHIPS - 1) * SENT)], msg_recv)
    half[c] = got[pl.ds(2, CHIPS, stride=8), :]
    swap = remote(half.at[c], half.at[c], core_send.at[0], core_recv.at[0], sibling, x)
    swap.start()
    slot_count = lax.broadcasted_iota(I32, (8, K), 1)
    for g in range(CHIPS // 8):
        s8 = slice(8 * g, 8 * g + 8)
        places = got[pl.ds(64 * g + 3, 8, stride=8), :].astype(I32)
        slots = got[pl.ds(64 * g + 4, 8, stride=8), :].astype(I32)
        lanes = slots >> 6
        picks = slots & (CHIPS - 1)
        for r, place in enumerate(((places & (2 * K - 1)) - 1, (places >> 8) - 1)):
            slot = place & (K - 1)
            slot_s[r, s8, :] = slot
            pick_s[r, s8, :] = jnp.where(place >= 0, jnp.take_along_axis(picks, slot, axis=1), -1)
        lane_s[s8, :] = lanes
        rank_s[s8, :] = jnp.where(jnp.take_along_axis(places >> 8, lanes, axis=1) == slot_count + 1, 1, 0)

    def scatter(n, into):
        def eight(j, carry):
            base = pl.multiple_of(j * 8, 8)
            sums = [[jnp.zeros((8, K), F32) for _ in range(8)] for _ in range(n)]
            for r in range(2):
                for g in range(CHIPS // 8):
                    p = pick_s[r, 8 * g : 8 * g + 8, :] - base
                    vals = [turn[r, f, 8 * g : 8 * g + 8, :] for f in range(n)]
                    for k in range(8):
                        hit = p == k
                        for f in range(n):
                            sums[f][k] = sums[f][k] + jnp.where(hit, vals[f], 0.0)
            for f in range(n):
                done = [jnp.sum(sums[f][k], axis=0, keepdims=True) for k in range(8)]
                into[pl.ds(pl.multiple_of(base + f * PICKS, 8), 8), :] = jnp.concatenate(done, axis=0)
            return carry

        lax.fori_loop(0, PICKS // 8, eight, 0)

    for g in range(CHIPS // 8):
        s8 = slice(8 * g, 8 * g + 8)
        vals = got[pl.ds(64 * g + 5, 8, stride=8), :]
        for r in range(2):
            turn[r, 0, s8, :] = jnp.take_along_axis(vals, slot_s[r, s8, :], axis=1)
    scatter(1, part.at[0])
    bound_swap = remote(
        part.at[0, pl.ds(0, PICKS)], bound_in, core_send.at[1], core_recv.at[1], sibling, x
    )
    bound_swap.start()
    swap.wait()
    table[...] = jnp.transpose(jnp.concatenate([half[0], half[1]], axis=0))
    bound_swap.wait()
    scale[...] = 1.0 / (1.0 + (part[0, 0:PICKS, :] + bound_in[...]))

    def gathered(f, g):
        s8 = slice(8 * g, 8 * g + 8)
        lanes = lane_s[s8, :]
        first_rank = jnp.take_along_axis(pick_rows(table, f * CHIPS, pick_s[0, s8, :]), lanes, axis=1)
        second_rank = jnp.take_along_axis(pick_rows(table, f * CHIPS, pick_s[1, s8, :]), lanes, axis=1)
        return jnp.where(rank_s[s8, :] == 0, first_rank, second_rank)

    def fetch(off, up, down):
        def one(i):
            arrived(off, i, up, down)
            unfolded(i, off, up, down)

        return one

    loop(LATE, RING, fetch(1, True, True))
    loop(0, RING, fetch(3, True, True))
    loop(0, RING // 2, fetch(4, True, False))
    loop(RING // 2, RING, fetch(4, False, True))

    sub8 = lax.broadcasted_iota(I32, (8, K), 0)

    def sweep(it, carry):
        for g in range(CHIPS // 8):
            s8 = slice(8 * g, 8 * g + 8)
            s0, s1 = gathered(0, g), gathered(1, g)
            h0, l0 = split(s0)
            h1, l1 = split(s1)
            extra = got[pl.ds(64 * g + 6, 8, stride=8), :]
            left = jnp.concatenate([h0, l0, h1, l1], axis=0)
            g0 = extra * s0 - got[pl.ds(64 * g, 8, stride=8), :]
            g1 = extra * s1 - got[pl.ds(64 * g + 1, 8, stride=8), :]
            for j in range(0, 8, 2):
                m = dot(left, jnp.concatenate([grams[8 * g + j], grams[8 * g + j + 1]], axis=1))
                f0, f1 = m[0:8] + m[8:16], m[16:24] + m[24:32]
                g0 = g0 + jnp.where(sub8 == j, f0[:, 0:K], jnp.where(sub8 == j + 1, f0[:, K:], 0.0))
                g1 = g1 + jnp.where(sub8 == j, f1[:, 0:K], jnp.where(sub8 == j + 1, f1[:, K:], 0.0))
            for r in range(2):
                slots = slot_s[r, s8, :]
                turn[r, 0, s8, :] = jnp.take_along_axis(g0, slots, axis=1)
                turn[r, 1, s8, :] = jnp.take_along_axis(g1, slots, axis=1)
        mine = part.at[it + 1]
        scatter(2, mine)
        trade = remote(mine, part_in.at[it], core_send.at[it + 2], core_recv.at[it + 2], sibling, x)
        trade.start()
        trade.wait()
        for f in range(2):
            total = part[it + 1, f * PICKS : (f + 1) * PICKS, :] + part_in[it, f * PICKS : (f + 1) * PICKS, :]
            rows = slice(f * CHIPS, f * CHIPS + PICKS)
            table[rows, :] = jnp.maximum(table[rows, :] - total * scale[...], 0.0)
        return carry

    lax.fori_loop(0, ITER_C, sweep, 0)

    for g in range(CHIPS // 8):
        for f in range(2):
            back[pl.ds(32 * g + f, 8, stride=4), :] = gathered(f, g)
    s_buf[...] = jnp.transpose(table[...])
    back[pl.ds(2, CHIPS, stride=4), :] = s_buf[pl.ds(pl.multiple_of(c * CHIPS, CHIPS), CHIPS), :]
    back[pl.ds(3, CHIPS, stride=4), :] = jnp.zeros((CHIPS, K), F32)

    away = [(rz, ry) for rz in range(RING) for ry in range(RING) if rz or ry]
    for rz, ry in sorted(away, key=lambda r: -min(r[0], RING - r[0]) - min(r[1], RING - r[1])):
        p = lax.rem(zc + rz, RING) * RING + lax.rem(yc + ry, RING)
        remote(
            back.at[pl.ds(pl.multiple_of(p * 4, 4), 4)],
            back_in.at[pl.ds(pl.multiple_of(q * 4, 4), 4)],
            back_send, back_recv, p * 2 + c, x,
        ).start()
    mine = pl.ds(pl.multiple_of(q * 4, 4), 4)
    own_back = pltpu.make_async_copy(back.at[mine], back_in.at[mine], here_sem.at[1])
    own_back.start()
    own_back.wait()
    drain(back_in.at[pl.ds(0, (CHIPS - 1) * 4)], back_recv)

    slot_traces = jnp.concatenate([back_in[pl.ds(0, CHIPS, stride=4), :], back_in[pl.ds(1, CHIPS, stride=4), :]], axis=0)
    hi, lo = split(slot_traces)
    s_all[x, :, 0:K] = hi
    s_all[x, :, K : 2 * K] = lo
    sends = []
    for i in range(1, XS):
        sends.append(remote(s_all.at[x], s_all.at[x], x_send.at[i], x_recv.at[i], me, lax.rem(x + i, XS)))
    for s in sends:
        s.start()

    held = back_in[pl.ds(2, CHIPS, stride=4), :]
    both = jnp.transpose(jnp.concatenate([held, pltpu.roll(held, CHIPS, 1)], axis=0))
    out_traces[0:PICKS, :] = both[0:PICKS]
    out_traces[PICKS:, :] = jnp.maximum(traces[PICKS:, :], 0.0)

    y_own.wait()
    for i in range(1, XS):
        remote(rec, y_all.at[x], y_send.at[i], y_recv.at[i], me, lax.rem(x + i, XS)).wait()
    for s in sends:
        s.wait()

    p_hi = jnp.zeros((K, K), F32)
    p_mix = jnp.zeros((K, K), F32)
    for i in range(XS):
        m = dot_t(s_all[i, :, 0:K], s_all[i])
        p_hi = p_hi + m[:, 0:K]
        p_mix = p_mix + m[:, K : 2 * K]
    p = p_hi + (p_mix + jnp.transpose(p_mix))
    step_row = 1.0 / (1.0 + jnp.sum(jnp.abs(p), axis=0, keepdims=True))
    w_hi, w_lo = split(p * step_row)
    w_buf[0:K, 0:K] = w_hi
    w_buf[0:K, K : 2 * K] = w_lo
    w_buf[K : 2 * K, 0:K] = w_hi
    w_buf[K : 2 * K, K : 2 * K] = jnp.zeros((K, K), BF16)
    for n in range(V // K):
        rows = slice(n * K, (n + 1) * K)
        total = dot(y_all[0, rows, :], s_all[0, :, 0:K])
        for i in range(1, XS):
            total = total + dot(y_all[i, rows, :], s_all[i, :, 0:K])
        start = foot[rows, :].astype(F32)
        q_buf[rows, :] = jnp.where(start > 0.0, total * step_row, -jnp.inf)
        x_buf[rows, :] = start

    def refine(n, carry):
        for k in range(V // ROWS):
            rows = slice(k * ROWS, (k + 1) * ROWS)
            cur = x_buf[rows, :]
            hi, lo = split(cur)
            m = dot(jnp.concatenate([hi, lo], axis=1), w_buf[...])
            moved = cur - (m[:, 0:K] + m[:, K : 2 * K]) + q_buf[rows, :]
            x_buf[rows, :] = jnp.maximum(moved, 0.0)
        return carry

    lax.fori_loop(0, ITER_A, refine, 0)
    out_foot[...] = x_buf[...].astype(BF16)

    drain(packed.at[pl.ds(0, CHIPS - 1)], gram_send)
    drain(msg.at[pl.ds(0, (CHIPS - 1) * SENT)], msg_send)
    drain(back.at[pl.ds(0, (CHIPS - 1) * 4)], back_send)


def body(recording, footprints, slot_owner, slot_pick, traces):
    vmem = pl.BlockSpec(memory_space=pltpu.VMEM)
    dma = pltpu.SemaphoreType.DMA
    return pl.pallas_call(
        kernel,
        out_shape=(
            jax.ShapeDtypeStruct(traces.shape, F32),
            jax.ShapeDtypeStruct(footprints.shape, BF16),
        ),
        in_specs=[pl.BlockSpec(memory_space=pltpu.HBM)] * 5,
        out_specs=(vmem, vmem),
        scratch_shapes=[
            pltpu.VMEM((V, K), BF16),
            pltpu.VMEM((V, K), BF16),
            pltpu.VMEM((1, K), I32),
            pltpu.VMEM((1, K), I32),
            pltpu.VMEM(traces.shape, F32),
            pltpu.VMEM((CHIPS, K, K), BF16),
            pltpu.VMEM((CHIPS, 3 * K // 4, K), BF16),
            pltpu.VMEM((CHIPS * 8, K), F32),
            pltpu.VMEM((CHIPS * 8, K), F32),
            pltpu.VMEM((2, CHIPS, K), F32),
            pltpu.VMEM((ITER_C + 1, 2 * PICKS, K), F32),
            pltpu.VMEM((ITER_C, 2 * PICKS, K), F32),
            pltpu.VMEM((PICKS, K), F32),
            pltpu.VMEM((K, K), F32),
            pltpu.VMEM((PICKS, K), F32),
            pltpu.VMEM((K, K), F32),
            pltpu.VMEM((CHIPS * 4, K), F32),
            pltpu.VMEM((CHIPS * 4, K), F32),
            pltpu.VMEM((XS, K, 2 * K), BF16),
            pltpu.VMEM((XS, V, K), BF16),
            pltpu.VMEM((V, K), F32),
            pltpu.VMEM((V, K), F32),
            pltpu.VMEM((2 * K, 2 * K), BF16),
            pltpu.VMEM((2, CHIPS, K), I32),
            pltpu.VMEM((2, CHIPS, K), I32),
            pltpu.VMEM((CHIPS, K), I32),
            pltpu.VMEM((CHIPS, K), I32),
            pltpu.VMEM((2, 2, CHIPS, K), F32),
            dma,
            dma((RING,)),
            dma((4, 2, RING)),
            dma,
            dma,
            dma((ITER_C + 2,)),
            dma((ITER_C + 2,)),
            dma,
            dma,
            dma((XS,)),
            dma((XS,)),
            dma((XS,)),
            dma((XS,)),
            dma((2,)),
            dma((5,)),
            pltpu.SemaphoreType.REGULAR,
        ],
        compiler_params=pltpu.CompilerParams(
            collective_id=0, has_side_effects=True, vmem_limit_bytes=40 << 20
        ),
    )(recording, footprints, slot_owner.reshape(1, K), slot_pick.reshape(1, K), traces)


def solution(mesh):
    in_specs = (P("tile", "frame"), P("tile", None), P("tile", None), P("tile"), P("tile", "frame"))
    out_specs = (P("tile", "frame"), P("tile", None))
    return jax.shard_map(body, mesh=mesh, in_specs=in_specs, out_specs=out_specs, check_vma=False)
```

```python
import jax
import jax.numpy as jnp
from jax import lax
from jax.experimental import pallas as pl
from jax.experimental.pallas import tpu as pltpu
from jax.sharding import PartitionSpec as P

ITER_C = 4
ITER_A = 8
LATE = 8
TELL = 7
SENT = 7
ROWS = 256
RING = 8
CHIPS = 64
XS = 4
PICKS = 40
K = 128
V = 1024
MESH = pl.DeviceIdType.MESH
F32 = jnp.float32
BF16 = jnp.bfloat16
I32 = jnp.int32


def dot(a, b):
    return jnp.dot(a, b, preferred_element_type=F32)


def dot_t(a, b):
    return lax.dot_general(a, b, (((0,), (0,)), ((), ())), preferred_element_type=F32)


def split(v):
    hi = v.astype(BF16)
    return hi, (v - hi.astype(F32)).astype(BF16)


def remote(src, dst, send, recv, tile, frame):
    return pltpu.make_async_remote_copy(
        src_ref=src, dst_ref=dst, send_sem=send, recv_sem=recv, device_id=(tile, frame), device_id_type=MESH
    )


def drain(ref, sem):
    pltpu.make_async_copy(ref, ref, sem).wait()


def ring_order(i):
    half = (i + 1) // 2
    return lax.rem(RING + half * (2 * (i % 2) - 1), RING)


def pick_rows(table, row, pick):
    low, high = jnp.bitwise_and(pick, 7), pick >> 3
    out = jnp.zeros(pick.shape, F32)
    for j in range(PICKS // 8):
        got = jnp.take_along_axis(table[row + 8 * j : row + 8 * j + 8, :], low, axis=0)
        out = jnp.where(high == j, got, out)
    return out


def kernel(
    rec_hbm, foot_hbm, owner_hbm, pick_hbm, traces_hbm,
    out_traces, out_foot,
    rec, foot, owner_in, pick_in, traces,
    grams, packed, msg, got, half, part, part_in, bound_in, table, scale, s_buf, back, back_in, s_all, y_all, x_buf, q_buf, w_buf,
    pick_s, slot_s, lane_s, rank_s, turn,
    gram_send, gram_one, gram_two, msg_send, msg_recv, core_send, core_recv, back_send, back_recv, x_send, x_recv, y_send, y_recv, here_sem, load_sem, ready,
):
    me = lax.axis_index("tile")
    x = lax.axis_index("frame")
    c = lax.rem(me, 2)
    q = me // 2
    zc, yc = q // RING, lax.rem(q, RING)
    sibling = me + 1 - 2 * c
    a = zc * (1 - c) + yc * c
    b = yc * (1 - c) + zc * c
    sa, sb = RING - (RING - 1) * c, 1 + (RING - 1) * c

    def ring_a(r):
        return (lax.rem(a + r, RING) * sa + b * sb) * 2 + c

    def ring_b(r):
        return (a * sa + lax.rem(b + r, RING) * sb) * 2 + c

    loads = [
        pltpu.make_async_copy(src, dst, load_sem.at[n])
        for n, (src, dst) in enumerate(
            ((foot_hbm, foot), (rec_hbm, rec), (owner_hbm, owner_in), (pick_hbm, pick_in), (traces_hbm, traces))
        )
    ]
    for load in loads:
        load.start()
    barrier = pltpu.get_barrier_semaphore()
    for r in (4, 3, 5, 2, 6, 1, 7):
        pl.semaphore_signal(barrier, inc=1, device_id=(ring_a(r), x), device_id_type=MESH)
        pl.semaphore_signal(barrier, inc=1, device_id=(ring_b(r), x), device_id_type=MESH)
    for i in range(1, XS):
        pl.semaphore_signal(barrier, inc=1, device_id=(me, lax.rem(x + i, XS)), device_id_type=MESH)
    pl.semaphore_signal(barrier, inc=1, device_id=(sibling, x), device_id_type=MESH)
    for load in loads:
        load.wait()

    block = foot[...]
    gram = dot_t(block, block)
    drive = dot_t(rec[...], block)
    grams[q] = gram.astype(BF16)
    right = lax.broadcasted_iota(I32, (K // 4, K), 1) >= K // 2
    fold = jnp.where(right, gram[K // 2 : 3 * K // 4], pltpu.roll(gram[3 * K // 4 :], K // 2, 1))
    packed[q, 0 : K // 2] = gram[0 : K // 2].astype(BF16)
    packed[q, K // 2 :] = fold.astype(BF16)
    bound = jnp.sum(jnp.abs(gram), axis=0, keepdims=True)
    lane = lax.broadcasted_iota(I32, (K, K), 1)
    sub = lax.broadcasted_iota(I32, (K, K), 0)
    rest = jnp.sum(jnp.where(lane == sub, gram - gram.astype(BF16).astype(F32), 0.0), axis=0, keepdims=True)
    own = owner_in[...]
    own = jnp.broadcast_to((own & 1) * CHIPS + (own >> 1), (K, K))
    own_t = jnp.transpose(own.astype(F32)).astype(I32)
    same = own == own_t
    rank_col = jnp.sum(jnp.where(same & (lane < sub), 1.0, 0.0), axis=1, keepdims=True)
    place = (sub + 1).astype(F32) * jnp.where(rank_col < 0.5, 1.0, 2.0 * K)
    slots_of = jnp.sum(jnp.where(own_t == lane, place, 0.0), axis=0, keepdims=True)
    slot_row = (own[0:1, :] * CHIPS + pick_in[...]).astype(F32)
    by_frame = jnp.transpose(traces[0:K, :])
    low_lane = lax.broadcasted_iota(I32, (CHIPS, K), 1) < CHIPS
    rows = (
        drive[0:CHIPS],
        drive[CHIPS:K],
        jnp.where(low_lane, by_frame[0:CHIPS], pltpu.roll(by_frame[CHIPS:K], CHIPS, 1)),
        jnp.broadcast_to(slots_of, (CHIPS, K)),
        jnp.broadcast_to(slot_row, (CHIPS, K)),
        jnp.broadcast_to(bound, (CHIPS, K)),
        jnp.broadcast_to(rest, (CHIPS, K)),
    )
    for j, row in enumerate(rows):
        msg[pl.ds(j, CHIPS, stride=8), :] = row
    for j, row in enumerate(rows):
        got[pl.ds(q * 8 + j, 1), :] = msg[pl.ds(q * 8 + j, 1), :]

    pl.semaphore_wait(barrier, 2 * (RING - 1) + XS)
    for r in (4, 3, 5, 2, 6, 1, 7):
        pl.semaphore_signal(ready, inc=1, device_id=(ring_b(r), x), device_id_type=MESH)

    def forward(i, off, hop, up=True, down=True):
        column = lax.rem(a + ring_order(i), RING) * sa
        if up:
            p = column + lax.rem(b + RING - off, RING) * sb
            remote(packed.at[p], packed.at[p], gram_send, gram_two.at[off + hop - 1, 0, i], ring_b(hop), x).start()
        if down:
            p = column + lax.rem(b + off, RING) * sb
            remote(packed.at[p], packed.at[p], gram_send, gram_two.at[off + hop - 1, 1, i], ring_b(RING - hop), x).start()

    def unfold(p):
        high = packed[p, 0 : K // 2]
        fold = packed[p, K // 2 :]
        grams[p, 0 : K // 2] = high
        grams[p, K // 2 : 3 * K // 4] = fold
        grams[p, 3 * K // 4 :] = pltpu.roll(fold.astype(F32), K // 2, 1).astype(BF16)
        grams[p, K // 2 :, 0 : K // 2] = jnp.transpose(high.astype(F32))[K // 2 :].astype(BF16)

    def unfolded(i, off, up=True, down=True):
        column = lax.rem(a + ring_order(i), RING) * sa
        if up:
            unfold(column + lax.rem(b + RING - off, RING) * sb)
        if down:
            unfold(column + lax.rem(b + off, RING) * sb)

    def arrived(off, i, up=True, down=True):
        if up:
            pltpu.make_async_copy(packed.at[0], packed.at[0], gram_two.at[off - 1, 0, i]).wait()
        if down:
            pltpu.make_async_copy(packed.at[0], packed.at[0], gram_two.at[off - 1, 1, i]).wait()

    def tell(n):
        rz, ry = ring_order(RING - 1 - n // RING), ring_order(RING - 1 - lax.rem(n, RING))
        p = lax.rem(zc + rz, RING) * RING + lax.rem(yc + ry, RING)
        remote(
            msg.at[pl.ds(pl.multiple_of(p * 8, 8), SENT)],
            got.at[pl.ds(pl.multiple_of(q * 8, 8), SENT)],
            msg_send, msg_recv, p * 2 + c, x,
        ).start()

    def loop(start, stop, step):
        def run(i, carry):
            step(i)
            return carry

        lax.fori_loop(start, stop, run, 0)

    forward(0, 0, 1)
    loop(1, RING, lambda i: remote(
        packed.at[q], packed.at[q], gram_send, gram_one.at[RING - i], ring_a(RING - ring_order(RING - i)), x
    ).start())
    for i in range(1, XS):
        remote(rec, y_all.at[x], y_send.at[i], y_recv.at[i], me, lax.rem(x + i, XS)).start()
    y_own = pltpu.make_async_copy(rec, y_all.at[x], here_sem.at[0])
    y_own.start()

    def pass_on(i):
        pltpu.make_async_copy(packed.at[0], packed.at[0], gram_one.at[i]).wait()
        forward(i, 0, 1)
        unfolded(i, 0, down=False)

    def some(n):
        loop(n * TELL, (n + 1) * TELL, tell)

    loop(1, 5, pass_on)
    pl.semaphore_wait(ready, RING - 1)

    def pass_and_tell(i):
        pass_on(i)
        loop((i - 5) * 9, (i - 5) * 9 + 9, tell)

    loop(5, RING, pass_and_tell)

    def pass_late(i):
        pass_on(i)
        forward(i, 0, 2)
        some(i - LATE)

    loop(LATE, RING, pass_late)

    def second(i):
        arrived(1, i)
        forward(i, 1, 1)
        loop(27 + (9 * i) // 2, 27 + (9 * i + 9) // 2, tell)
        unfolded(i, 1)

    loop(0, LATE, second)

    def third_up(i):
        arrived(2, i)
        forward(i, 2, 1)
        forward(i, 2, 2, down=False)
        unfolded(i, 2)

    def third_down(i):
        arrived(2, i)
        forward(i, 2, 1)
        forward(i, 2, 2, up=False)
        unfolded(i, 2)

    loop(0, RING // 2, third_up)
    loop(RING // 2, RING, third_down)

    drain(got.at[pl.ds(0, (CHIPS - 1) * SENT)], msg_recv)
    half[c] = got[pl.ds(2, CHIPS, stride=8), :]
    swap = remote(half.at[c], half.at[c], core_send.at[0], core_recv.at[0], sibling, x)
    swap.start()
    slot_count = lax.broadcasted_iota(I32, (8, K), 1)
    for g in range(CHIPS // 8):
        s8 = slice(8 * g, 8 * g + 8)
        places = got[pl.ds(64 * g + 3, 8, stride=8), :].astype(I32)
        slots = got[pl.ds(64 * g + 4, 8, stride=8), :].astype(I32)
        lanes = slots >> 6
        picks = slots & (CHIPS - 1)
        for r, place in enumerate(((places & (2 * K - 1)) - 1, (places >> 8) - 1)):
            slot = place & (K - 1)
            slot_s[r, s8, :] = slot
            pick_s[r, s8, :] = jnp.where(place >= 0, jnp.take_along_axis(picks, slot, axis=1), -1)
        lane_s[s8, :] = lanes
        rank_s[s8, :] = jnp.where(jnp.take_along_axis(places >> 8, lanes, axis=1) == slot_count + 1, 1, 0)

    def scatter(n, into):
        def eight(j, carry):
            base = pl.multiple_of(j * 8, 8)
            sums = [[jnp.zeros((8, K), F32) for _ in range(8)] for _ in range(n)]
            for r in range(2):
                for g in range(CHIPS // 8):
                    p = pick_s[r, 8 * g : 8 * g + 8, :] - base
                    vals = [turn[r, f, 8 * g : 8 * g + 8, :] for f in range(n)]
                    for k in range(8):
                        hit = p == k
                        for f in range(n):
                            sums[f][k] = sums[f][k] + jnp.where(hit, vals[f], 0.0)
            for f in range(n):
                done = [jnp.sum(sums[f][k], axis=0, keepdims=True) for k in range(8)]
                into[pl.ds(pl.multiple_of(base + f * PICKS, 8), 8), :] = jnp.concatenate(done, axis=0)
            return carry

        lax.fori_loop(0, PICKS // 8, eight, 0)

    for g in range(CHIPS // 8):
        s8 = slice(8 * g, 8 * g + 8)
        vals = got[pl.ds(64 * g + 5, 8, stride=8), :]
        for r in range(2):
            turn[r, 0, s8, :] = jnp.take_along_axis(vals, slot_s[r, s8, :], axis=1)
    scatter(1, part.at[0])
    bound_swap = remote(
        part.at[0, pl.ds(0, PICKS)], bound_in, core_send.at[1], core_recv.at[1], sibling, x
    )
    bound_swap.start()
    swap.wait()
    table[...] = jnp.transpose(jnp.concatenate([half[0], half[1]], axis=0))
    bound_swap.wait()
    scale[...] = 1.0 / (1.0 + (part[0, 0:PICKS, :] + bound_in[...]))

    def gathered(f, g):
        s8 = slice(8 * g, 8 * g + 8)
        lanes = lane_s[s8, :]
        first_rank = jnp.take_along_axis(pick_rows(table, f * CHIPS, pick_s[0, s8, :]), lanes, axis=1)
        second_rank = jnp.take_along_axis(pick_rows(table, f * CHIPS, pick_s[1, s8, :]), lanes, axis=1)
        return jnp.where(rank_s[s8, :] == 0, first_rank, second_rank)

    def fetch(off, up, down):
        def one(i):
            arrived(off, i, up, down)
            unfolded(i, off, up, down)

        return one

    loop(LATE, RING, fetch(1, True, True))
    loop(0, RING, fetch(3, True, True))
    loop(0, RING // 2, fetch(4, True, False))
    loop(RING // 2, RING, fetch(4, False, True))

    sub8 = lax.broadcasted_iota(I32, (8, K), 0)

    def sweep(it, carry):
        for g in range(CHIPS // 8):
            s8 = slice(8 * g, 8 * g + 8)
            s0, s1 = gathered(0, g), gathered(1, g)
            h0, l0 = split(s0)
            h1, l1 = split(s1)
            extra = got[pl.ds(64 * g + 6, 8, stride=8), :]
            left = jnp.concatenate([h0, l0, h1, l1], axis=0)
            g0 = extra * s0 - got[pl.ds(64 * g, 8, stride=8), :]
            g1 = extra * s1 - got[pl.ds(64 * g + 1, 8, stride=8), :]
            for j in range(0, 8, 2):
                m = dot(left, jnp.concatenate([grams[8 * g + j], grams[8 * g + j + 1]], axis=1))
                f0, f1 = m[0:8] + m[8:16], m[16:24] + m[24:32]
                g0 = g0 + jnp.where(sub8 == j, f0[:, 0:K], jnp.where(sub8 == j + 1, f0[:, K:], 0.0))
                g1 = g1 + jnp.where(sub8 == j, f1[:, 0:K], jnp.where(sub8 == j + 1, f1[:, K:], 0.0))
            for r in range(2):
                slots = slot_s[r, s8, :]
                turn[r, 0, s8, :] = jnp.take_along_axis(g0, slots, axis=1)
                turn[r, 1, s8, :] = jnp.take_along_axis(g1, slots, axis=1)
        mine = part.at[it + 1]
        scatter(2, mine)
        trade = remote(mine, part_in.at[it], core_send.at[it + 2], core_recv.at[it + 2], sibling, x)
        trade.start()
        trade.wait()
        for f in range(2):
            total = part[it + 1, f * PICKS : (f + 1) * PICKS, :] + part_in[it, f * PICKS : (f + 1) * PICKS, :]
            rows = slice(f * CHIPS, f * CHIPS + PICKS)
            table[rows, :] = jnp.maximum(table[rows, :] - total * scale[...], 0.0)
        return carry

    lax.fori_loop(0, ITER_C, sweep, 0)

    for g in range(CHIPS // 8):
        for f in range(2):
            back[pl.ds(32 * g + f, 8, stride=4), :] = gathered(f, g)
    s_buf[...] = jnp.transpose(table[...])
    back[pl.ds(2, CHIPS, stride=4), :] = s_buf[pl.ds(pl.multiple_of(c * CHIPS, CHIPS), CHIPS), :]
    back[pl.ds(3, CHIPS, stride=4), :] = jnp.zeros((CHIPS, K), F32)

    away = [(rz, ry) for rz in range(RING) for ry in range(RING) if rz or ry]
    for rz, ry in sorted(away, key=lambda r: -min(r[0], RING - r[0]) - min(r[1], RING - r[1])):
        p = lax.rem(zc + rz, RING) * RING + lax.rem(yc + ry, RING)
        remote(
            back.at[pl.ds(pl.multiple_of(p * 4, 4), 4)],
            back_in.at[pl.ds(pl.multiple_of(q * 4, 4), 4)],
            back_send, back_recv, p * 2 + c, x,
        ).start()
    mine = pl.ds(pl.multiple_of(q * 4, 4), 4)
    own_back = pltpu.make_async_copy(back.at[mine], back_in.at[mine], here_sem.at[1])
    own_back.start()
    own_back.wait()
    drain(back_in.at[pl.ds(0, (CHIPS - 1) * 4)], back_recv)

    slot_traces = jnp.concatenate([back_in[pl.ds(0, CHIPS, stride=4), :], back_in[pl.ds(1, CHIPS, stride=4), :]], axis=0)
    hi, lo = split(slot_traces)
    s_all[x, :, 0:K] = hi
    s_all[x, :, K : 2 * K] = lo
    sends = []
    for i in range(1, XS):
        sends.append(remote(s_all.at[x], s_all.at[x], x_send.at[i], x_recv.at[i], me, lax.rem(x + i, XS)))
    for s in sends:
        s.start()

    held = back_in[pl.ds(2, CHIPS, stride=4), :]
    both = jnp.transpose(jnp.concatenate([held, pltpu.roll(held, CHIPS, 1)], axis=0))
    out_traces[0:PICKS, :] = both[0:PICKS]
    out_traces[PICKS:, :] = jnp.maximum(traces[PICKS:, :], 0.0)

    y_own.wait()
    for i in range(1, XS):
        remote(rec, y_all.at[x], y_send.at[i], y_recv.at[i], me, lax.rem(x + i, XS)).wait()
    for s in sends:
        s.wait()

    p_hi = jnp.zeros((K, K), F32)
    p_mix = jnp.zeros((K, K), F32)
    for i in range(XS):
        m = dot_t(s_all[i, :, 0:K], s_all[i])
        p_hi = p_hi + m[:, 0:K]
        p_mix = p_mix + m[:, K : 2 * K]
    p = p_hi + (p_mix + jnp.transpose(p_mix))
    step_row = 1.0 / (1.0 + jnp.sum(jnp.abs(p), axis=0, keepdims=True))
    w_hi, w_lo = split(p * step_row)
    w_buf[0:K, 0:K] = w_hi
    w_buf[0:K, K : 2 * K] = w_lo
    w_buf[K : 2 * K, 0:K] = w_hi
    w_buf[K : 2 * K, K : 2 * K] = jnp.zeros((K, K), BF16)
    for n in range(V // K):
        rows = slice(n * K, (n + 1) * K)
        total = dot(y_all[0, rows, :], s_all[0, :, 0:K])
        for i in range(1, XS):
            total = total + dot(y_all[i, rows, :], s_all[i, :, 0:K])
        start = foot[rows, :].astype(F32)
        q_buf[rows, :] = jnp.where(start > 0.0, total * step_row, -jnp.inf)
        x_buf[rows, :] = start

    def refine(n, carry):
        for k in range(V // ROWS):
            rows = slice(k * ROWS, (k + 1) * ROWS)
            cur = x_buf[rows, :]
            hi, lo = split(cur)
            m = dot(jnp.concatenate([hi, lo], axis=1), w_buf[...])
            moved = cur - (m[:, 0:K] + m[:, K : 2 * K]) + q_buf[rows, :]
            x_buf[rows, :] = jnp.maximum(moved, 0.0)
        return carry

    lax.fori_loop(0, ITER_A, refine, 0)
    out_foot[...] = x_buf[...].astype(BF16)

    drain(packed.at[pl.ds(0, CHIPS - 1)], gram_send)
    drain(msg.at[pl.ds(0, (CHIPS - 1) * SENT)], msg_send)
    drain(back.at[pl.ds(0, (CHIPS - 1) * 4)], back_send)


def body(recording, footprints, slot_owner, slot_pick, traces):
    vmem = pl.BlockSpec(memory_space=pltpu.VMEM)
    dma = pltpu.SemaphoreType.DMA
    return pl.pallas_call(
        kernel,
        out_shape=(
            jax.ShapeDtypeStruct(traces.shape, F32),
            jax.ShapeDtypeStruct(footprints.shape, BF16),
        ),
        in_specs=[pl.BlockSpec(memory_space=pltpu.HBM)] * 5,
        out_specs=(vmem, vmem),
        scratch_shapes=[
            pltpu.VMEM((V, K), BF16),
            pltpu.VMEM((V, K), BF16),
            pltpu.VMEM((1, K), I32),
            pltpu.VMEM((1, K), I32),
            pltpu.VMEM(traces.shape, F32),
            pltpu.VMEM((CHIPS, K, K), BF16),
            pltpu.VMEM((CHIPS, 3 * K // 4, K), BF16),
            pltpu.VMEM((CHIPS * 8, K), F32),
            pltpu.VMEM((CHIPS * 8, K), F32),
            pltpu.VMEM((2, CHIPS, K), F32),
            pltpu.VMEM((ITER_C + 1, 2 * PICKS, K), F32),
            pltpu.VMEM((ITER_C, 2 * PICKS, K), F32),
            pltpu.VMEM((PICKS, K), F32),
            pltpu.VMEM((K, K), F32),
            pltpu.VMEM((PICKS, K), F32),
            pltpu.VMEM((K, K), F32),
            pltpu.VMEM((CHIPS * 4, K), F32),
            pltpu.VMEM((CHIPS * 4, K), F32),
            pltpu.VMEM((XS, K, 2 * K), BF16),
            pltpu.VMEM((XS, V, K), BF16),
            pltpu.VMEM((V, K), F32),
            pltpu.VMEM((V, K), F32),
            pltpu.VMEM((2 * K, 2 * K), BF16),
            pltpu.VMEM((2, CHIPS, K), I32),
            pltpu.VMEM((2, CHIPS, K), I32),
            pltpu.VMEM((CHIPS, K), I32),
            pltpu.VMEM((CHIPS, K), I32),
            pltpu.VMEM((2, 2, CHIPS, K), F32),
            dma,
            dma((RING,)),
            dma((4, 2, RING)),
            dma,
            dma,
            dma((ITER_C + 2,)),
            dma((ITER_C + 2,)),
            dma,
            dma,
            dma((XS,)),
            dma((XS,)),
            dma((XS,)),
            dma((XS,)),
            dma((2,)),
            dma((5,)),
            pltpu.SemaphoreType.REGULAR,
        ],
        compiler_params=pltpu.CompilerParams(
            collective_id=0, has_side_effects=True, vmem_limit_bytes=40 << 20
        ),
    )(recording, footprints, slot_owner.reshape(1, K), slot_pick.reshape(1, K), traces)


def solution(mesh):
    in_specs = (P("tile", "frame"), P("tile", None), P("tile", None), P("tile"), P("tile", "frame"))
    out_specs = (P("tile", "frame"), P("tile", None))
    return jax.shard_map(body, mesh=mesh, in_specs=in_specs, out_specs=out_specs, check_vma=False)
```

```python
import jax
import jax.numpy as jnp
from jax import lax
from jax.experimental import pallas as pl
from jax.experimental.pallas import tpu as pltpu
from jax.sharding import PartitionSpec as P

ITER_C = 4
ITER_A = 8
LATE = 8
TELL = 7
SENT = 7
ROWS = 256
RING = 8
CHIPS = 64
XS = 4
PICKS = 40
K = 128
V = 1024
MESH = pl.DeviceIdType.MESH
F32 = jnp.float32
BF16 = jnp.bfloat16
I32 = jnp.int32


def dot(a, b):
    return jnp.dot(a, b, preferred_element_type=F32)


def dot_t(a, b):
    return lax.dot_general(a, b, (((0,), (0,)), ((), ())), preferred_element_type=F32)


def split(v):
    hi = v.astype(BF16)
    return hi, (v - hi.astype(F32)).astype(BF16)


def remote(src, dst, send, recv, tile, frame):
    return pltpu.make_async_remote_copy(
        src_ref=src, dst_ref=dst, send_sem=send, recv_sem=recv, device_id=(tile, frame), device_id_type=MESH
    )


def drain(ref, sem):
    pltpu.make_async_copy(ref, ref, sem).wait()


def ring_order(i):
    half = (i + 1) // 2
    return lax.rem(RING + half * (2 * (i % 2) - 1), RING)


def pick_rows(table, row, pick):
    low, high = jnp.bitwise_and(pick, 7), pick >> 3
    out = jnp.zeros(pick.shape, F32)
    for j in range(PICKS // 8):
        got = jnp.take_along_axis(table[row + 8 * j : row + 8 * j + 8, :], low, axis=0)
        out = jnp.where(high == j, got, out)
    return out


def kernel(
    rec_hbm, foot_hbm, owner_hbm, pick_hbm, traces_hbm,
    out_traces, out_foot,
    rec, foot, owner_in, pick_in, traces,
    grams, packed, msg, got, half, part, part_in, bound_in, table, scale, s_buf, back, back_in, s_all, y_all, x_buf, q_buf, w_buf,
    pick_s, slot_s, lane_s, rank_s, turn,
    gram_send, gram_one, gram_two, msg_send, msg_recv, core_send, core_recv, back_send, back_recv, x_send, x_recv, y_send, y_recv, here_sem, load_sem, ready,
):
    me = lax.axis_index("tile")
    x = lax.axis_index("frame")
    c = lax.rem(me, 2)
    q = me // 2
    zc, yc = q // RING, lax.rem(q, RING)
    sibling = me + 1 - 2 * c
    a = zc * (1 - c) + yc * c
    b = yc * (1 - c) + zc * c
    sa, sb = RING - (RING - 1) * c, 1 + (RING - 1) * c

    def ring_a(r):
        return (lax.rem(a + r, RING) * sa + b * sb) * 2 + c

    def ring_b(r):
        return (a * sa + lax.rem(b + r, RING) * sb) * 2 + c

    loads = [
        pltpu.make_async_copy(src, dst, load_sem.at[n])
        for n, (src, dst) in enumerate(
            ((foot_hbm, foot), (rec_hbm, rec), (owner_hbm, owner_in), (pick_hbm, pick_in), (traces_hbm, traces))
        )
    ]
    for load in loads:
        load.start()
    barrier = pltpu.get_barrier_semaphore()
    for r in (4, 3, 5, 2, 6, 1, 7):
        pl.semaphore_signal(barrier, inc=1, device_id=(ring_a(r), x), device_id_type=MESH)
        pl.semaphore_signal(barrier, inc=1, device_id=(ring_b(r), x), device_id_type=MESH)
    for i in range(1, XS):
        pl.semaphore_signal(barrier, inc=1, device_id=(me, lax.rem(x + i, XS)), device_id_type=MESH)
    pl.semaphore_signal(barrier, inc=1, device_id=(sibling, x), device_id_type=MESH)
    for load in loads:
        load.wait()

    block = foot[...]
    gram = dot_t(block, block)
    drive = dot_t(rec[...], block)
    grams[q] = gram.astype(BF16)
    right = lax.broadcasted_iota(I32, (K // 4, K), 1) >= K // 2
    fold = jnp.where(right, gram[K // 2 : 3 * K // 4], pltpu.roll(gram[3 * K // 4 :], K // 2, 1))
    packed[q, 0 : K // 2] = gram[0 : K // 2].astype(BF16)
    packed[q, K // 2 :] = fold.astype(BF16)
    bound = jnp.sum(jnp.abs(gram), axis=0, keepdims=True)
    lane = lax.broadcasted_iota(I32, (K, K), 1)
    sub = lax.broadcasted_iota(I32, (K, K), 0)
    rest = jnp.sum(jnp.where(lane == sub, gram - gram.astype(BF16).astype(F32), 0.0), axis=0, keepdims=True)
    own = owner_in[...]
    own = jnp.broadcast_to((own & 1) * CHIPS + (own >> 1), (K, K))
    own_t = jnp.transpose(own.astype(F32)).astype(I32)
    same = own == own_t
    rank_col = jnp.sum(jnp.where(same & (lane < sub), 1.0, 0.0), axis=1, keepdims=True)
    place = (sub + 1).astype(F32) * jnp.where(rank_col < 0.5, 1.0, 2.0 * K)
    slots_of = jnp.sum(jnp.where(own_t == lane, place, 0.0), axis=0, keepdims=True)
    slot_row = (own[0:1, :] * CHIPS + pick_in[...]).astype(F32)
    by_frame = jnp.transpose(traces[0:K, :])
    low_lane = lax.broadcasted_iota(I32, (CHIPS, K), 1) < CHIPS
    rows = (
        drive[0:CHIPS],
        drive[CHIPS:K],
        jnp.where(low_lane, by_frame[0:CHIPS], pltpu.roll(by_frame[CHIPS:K], CHIPS, 1)),
        jnp.broadcast_to(slots_of, (CHIPS, K)),
        jnp.broadcast_to(slot_row, (CHIPS, K)),
        jnp.broadcast_to(bound, (CHIPS, K)),
        jnp.broadcast_to(rest, (CHIPS, K)),
    )
    for j, row in enumerate(rows):
        msg[pl.ds(j, CHIPS, stride=8), :] = row
    for j, row in enumerate(rows):
        got[pl.ds(q * 8 + j, 1), :] = msg[pl.ds(q * 8 + j, 1), :]

    pl.semaphore_wait(barrier, 2 * (RING - 1) + XS)
    for r in (4, 3, 5, 2, 6, 1, 7):
        pl.semaphore_signal(ready, inc=1, device_id=(ring_b(r), x), device_id_type=MESH)

    def forward(i, off, hop, up=True, down=True):
        column = lax.rem(a + ring_order(i), RING) * sa
        if up:
            p = column + lax.rem(b + RING - off, RING) * sb
            remote(packed.at[p], packed.at[p], gram_send, gram_two.at[off + hop - 1, 0, i], ring_b(hop), x).start()
        if down:
            p = column + lax.rem(b + off, RING) * sb
            remote(packed.at[p], packed.at[p], gram_send, gram_two.at[off + hop - 1, 1, i], ring_b(RING - hop), x).start()

    def unfold(p):
        high = packed[p, 0 : K // 2]
        fold = packed[p, K // 2 :]
        grams[p, 0 : K // 2] = high
        grams[p, K // 2 : 3 * K // 4] = fold
        grams[p, 3 * K // 4 :] = pltpu.roll(fold.astype(F32), K // 2, 1).astype(BF16)
        grams[p, K // 2 :, 0 : K // 2] = jnp.transpose(high.astype(F32))[K // 2 :].astype(BF16)

    def unfolded(i, off, up=True, down=True):
        column = lax.rem(a + ring_order(i), RING) * sa
        if up:
            unfold(column + lax.rem(b + RING - off, RING) * sb)
        if down:
            unfold(column + lax.rem(b + off, RING) * sb)

    def arrived(off, i, up=True, down=True):
        if up:
            pltpu.make_async_copy(packed.at[0], packed.at[0], gram_two.at[off - 1, 0, i]).wait()
        if down:
            pltpu.make_async_copy(packed.at[0], packed.at[0], gram_two.at[off - 1, 1, i]).wait()

    def tell(n):
        rz, ry = ring_order(RING - 1 - n // RING), ring_order(RING - 1 - lax.rem(n, RING))
        p = lax.rem(zc + rz, RING) * RING + lax.rem(yc + ry, RING)
        remote(
            msg.at[pl.ds(pl.multiple_of(p * 8, 8), SENT)],
            got.at[pl.ds(pl.multiple_of(q * 8, 8), SENT)],
            msg_send, msg_recv, p * 2 + c, x,
        ).start()

    def loop(start, stop, step):
        def run(i, carry):
            step(i)
            return carry

        lax.fori_loop(start, stop, run, 0)

    forward(0, 0, 1)
    loop(1, RING, lambda i: remote(
        packed.at[q], packed.at[q], gram_send, gram_one.at[RING - i], ring_a(RING - ring_order(RING - i)), x
    ).start())
    for i in range(1, XS):
        remote(rec, y_all.at[x], y_send.at[i], y_recv.at[i], me, lax.rem(x + i, XS)).start()
    y_own = pltpu.make_async_copy(rec, y_all.at[x], here_sem.at[0])
    y_own.start()

    def pass_on(i):
        pltpu.make_async_copy(packed.at[0], packed.at[0], gram_one.at[i]).wait()
        forward(i, 0, 1)
        unfolded(i, 0, down=False)

    def some(n):
        loop(n * TELL, (n + 1) * TELL, tell)

    loop(1, 5, pass_on)
    pl.semaphore_wait(ready, RING - 1)

    def pass_and_tell(i):
        pass_on(i)
        loop((i - 5) * 9, (i - 5) * 9 + 9, tell)

    loop(5, RING, pass_and_tell)

    def pass_late(i):
        pass_on(i)
        forward(i, 0, 2)
        some(i - LATE)

    loop(LATE, RING, pass_late)

    def second(i):
        arrived(1, i)
        forward(i, 1, 1)
        loop(27 + (9 * i) // 2, 27 + (9 * i + 9) // 2, tell)
        unfolded(i, 1)

    loop(0, LATE, second)

    def third_up(i):
        arrived(2, i)
        forward(i, 2, 1)
        forward(i, 2, 2, down=False)
        unfolded(i, 2)

    def third_down(i):
        arrived(2, i)
        forward(i, 2, 1)
        forward(i, 2, 2, up=False)
        unfolded(i, 2)

    loop(0, RING // 2, third_up)
    loop(RING // 2, RING, third_down)

    drain(got.at[pl.ds(0, (CHIPS - 1) * SENT)], msg_recv)
    half[c] = got[pl.ds(2, CHIPS, stride=8), :]
    swap = remote(half.at[c], half.at[c], core_send.at[0], core_recv.at[0], sibling, x)
    swap.start()
    slot_count = lax.broadcasted_iota(I32, (8, K), 1)
    for g in range(CHIPS // 8):
        s8 = slice(8 * g, 8 * g + 8)
        places = got[pl.ds(64 * g + 3, 8, stride=8), :].astype(I32)
        slots = got[pl.ds(64 * g + 4, 8, stride=8), :].astype(I32)
        lanes = slots >> 6
        picks = slots & (CHIPS - 1)
        for r, place in enumerate(((places & (2 * K - 1)) - 1, (places >> 8) - 1)):
            slot = place & (K - 1)
            slot_s[r, s8, :] = slot
            pick_s[r, s8, :] = jnp.where(place >= 0, jnp.take_along_axis(picks, slot, axis=1), -1)
        lane_s[s8, :] = lanes
        rank_s[s8, :] = jnp.where(jnp.take_along_axis(places >> 8, lanes, axis=1) == slot_count + 1, 1, 0)

    def scatter(n, into):
        def eight(j, carry):
            base = pl.multiple_of(j * 8, 8)
            sums = [[jnp.zeros((8, K), F32) for _ in range(8)] for _ in range(n)]
            for r in range(2):
                for g in range(CHIPS // 8):
                    p = pick_s[r, 8 * g : 8 * g + 8, :] - base
                    vals = [turn[r, f, 8 * g : 8 * g + 8, :] for f in range(n)]
                    for k in range(8):
                        hit = p == k
                        for f in range(n):
                            sums[f][k] = sums[f][k] + jnp.where(hit, vals[f], 0.0)
            for f in range(n):
                done = [jnp.sum(sums[f][k], axis=0, keepdims=True) for k in range(8)]
                into[pl.ds(pl.multiple_of(base + f * PICKS, 8), 8), :] = jnp.concatenate(done, axis=0)
            return carry

        lax.fori_loop(0, PICKS // 8, eight, 0)

    for g in range(CHIPS // 8):
        s8 = slice(8 * g, 8 * g + 8)
        vals = got[pl.ds(64 * g + 5, 8, stride=8), :]
        for r in range(2):
            turn[r, 0, s8, :] = jnp.take_along_axis(vals, slot_s[r, s8, :], axis=1)
    scatter(1, part.at[0])
    bound_swap = remote(
        part.at[0, pl.ds(0, PICKS)], bound_in, core_send.at[1], core_recv.at[1], sibling, x
    )
    bound_swap.start()
    swap.wait()
    table[...] = jnp.transpose(jnp.concatenate([half[0], half[1]], axis=0))
    bound_swap.wait()
    scale[...] = 1.0 / (1.0 + (part[0, 0:PICKS, :] + bound_in[...]))

    def gathered(f, g):
        s8 = slice(8 * g, 8 * g + 8)
        lanes = lane_s[s8, :]
        first_rank = jnp.take_along_axis(pick_rows(table, f * CHIPS, pick_s[0, s8, :]), lanes, axis=1)
        second_rank = jnp.take_along_axis(pick_rows(table, f * CHIPS, pick_s[1, s8, :]), lanes, axis=1)
        return jnp.where(rank_s[s8, :] == 0, first_rank, second_rank)

    def fetch(off, up, down):
        def one(i):
            arrived(off, i, up, down)
            unfolded(i, off, up, down)

        return one

    loop(LATE, RING, fetch(1, True, True))
    loop(0, RING, fetch(3, True, True))
    loop(0, RING // 2, fetch(4, True, False))
    loop(RING // 2, RING, fetch(4, False, True))

    sub8 = lax.broadcasted_iota(I32, (8, K), 0)

    def sweep(it, carry):
        for g in range(CHIPS // 8):
            s8 = slice(8 * g, 8 * g + 8)
            s0, s1 = gathered(0, g), gathered(1, g)
            h0, l0 = split(s0)
            h1, l1 = split(s1)
            extra = got[pl.ds(64 * g + 6, 8, stride=8), :]
            left = jnp.concatenate([h0, l0, h1, l1], axis=0)
            g0 = extra * s0 - got[pl.ds(64 * g, 8, stride=8), :]
            g1 = extra * s1 - got[pl.ds(64 * g + 1, 8, stride=8), :]
            for j in range(0, 8, 2):
                m = dot(left, jnp.concatenate([grams[8 * g + j], grams[8 * g + j + 1]], axis=1))
                f0, f1 = m[0:8] + m[8:16], m[16:24] + m[24:32]
                g0 = g0 + jnp.where(sub8 == j, f0[:, 0:K], jnp.where(sub8 == j + 1, f0[:, K:], 0.0))
                g1 = g1 + jnp.where(sub8 == j, f1[:, 0:K], jnp.where(sub8 == j + 1, f1[:, K:], 0.0))
            for r in range(2):
                slots = slot_s[r, s8, :]
                turn[r, 0, s8, :] = jnp.take_along_axis(g0, slots, axis=1)
                turn[r, 1, s8, :] = jnp.take_along_axis(g1, slots, axis=1)
        mine = part.at[it + 1]
        scatter(2, mine)
        trade = remote(mine, part_in.at[it], core_send.at[it + 2], core_recv.at[it + 2], sibling, x)
        trade.start()
        trade.wait()
        for f in range(2):
            total = part[it + 1, f * PICKS : (f + 1) * PICKS, :] + part_in[it, f * PICKS : (f + 1) * PICKS, :]
            rows = slice(f * CHIPS, f * CHIPS + PICKS)
            table[rows, :] = jnp.maximum(table[rows, :] - total * scale[...], 0.0)
        return carry

    lax.fori_loop(0, ITER_C, sweep, 0)

    for g in range(CHIPS // 8):
        for f in range(2):
            back[pl.ds(32 * g + f, 8, stride=4), :] = gathered(f, g)
    s_buf[...] = jnp.transpose(table[...])
    back[pl.ds(2, CHIPS, stride=4), :] = s_buf[pl.ds(pl.multiple_of(c * CHIPS, CHIPS), CHIPS), :]

    away = [(rz, ry) for rz in range(RING) for ry in range(RING) if rz or ry]
    for rz, ry in sorted(away, key=lambda r: -min(r[0], RING - r[0]) - min(r[1], RING - r[1])):
        p = lax.rem(zc + rz, RING) * RING + lax.rem(yc + ry, RING)
        remote(
            back.at[pl.ds(pl.multiple_of(p * 4, 4), 3)],
            back_in.at[pl.ds(pl.multiple_of(q * 4, 4), 3)],
            back_send, back_recv, p * 2 + c, x,
        ).start()
    mine = pl.ds(pl.multiple_of(q * 4, 4), 3)
    own_back = pltpu.make_async_copy(back.at[mine], back_in.at[mine], here_sem.at[1])
    own_back.start()
    own_back.wait()
    drain(back_in.at[pl.ds(0, (CHIPS - 1) * 3)], back_recv)

    slot_traces = jnp.concatenate([back_in[pl.ds(0, CHIPS, stride=4), :], back_in[pl.ds(1, CHIPS, stride=4), :]], axis=0)
    hi, lo = split(slot_traces)
    s_all[x, :, 0:K] = hi
    s_all[x, :, K : 2 * K] = lo
    sends = []
    for i in range(1, XS):
        sends.append(remote(s_all.at[x], s_all.at[x], x_send.at[i], x_recv.at[i], me, lax.rem(x + i, XS)))
    for s in sends:
        s.start()

    held = back_in[pl.ds(2, CHIPS, stride=4), :]
    both = jnp.transpose(jnp.concatenate([held, pltpu.roll(held, CHIPS, 1)], axis=0))
    out_traces[0:PICKS, :] = both[0:PICKS]
    out_traces[PICKS:, :] = jnp.maximum(traces[PICKS:, :], 0.0)

    y_own.wait()
    for i in range(1, XS):
        remote(rec, y_all.at[x], y_send.at[i], y_recv.at[i], me, lax.rem(x + i, XS)).wait()
    for s in sends:
        s.wait()

    p_hi = jnp.zeros((K, K), F32)
    p_mix = jnp.zeros((K, K), F32)
    for i in range(XS):
        m = dot_t(s_all[i, :, 0:K], s_all[i])
        p_hi = p_hi + m[:, 0:K]
        p_mix = p_mix + m[:, K : 2 * K]
    p = p_hi + (p_mix + jnp.transpose(p_mix))
    step_row = 1.0 / (1.0 + jnp.sum(jnp.abs(p), axis=0, keepdims=True))
    w_hi, w_lo = split(p * step_row)
    w_buf[0:K, 0:K] = w_hi
    w_buf[0:K, K : 2 * K] = w_lo
    w_buf[K : 2 * K, 0:K] = w_hi
    w_buf[K : 2 * K, K : 2 * K] = jnp.zeros((K, K), BF16)
    for n in range(V // K):
        rows = slice(n * K, (n + 1) * K)
        total = dot(y_all[0, rows, :], s_all[0, :, 0:K])
        for i in range(1, XS):
            total = total + dot(y_all[i, rows, :], s_all[i, :, 0:K])
        start = foot[rows, :].astype(F32)
        q_buf[rows, :] = jnp.where(start > 0.0, total * step_row, -jnp.inf)
        x_buf[rows, :] = start

    def refine(n, carry):
        for k in range(V // ROWS):
            rows = slice(k * ROWS, (k + 1) * ROWS)
            cur = x_buf[rows, :]
            hi, lo = split(cur)
            m = dot(jnp.concatenate([hi, lo], axis=1), w_buf[...])
            moved = cur - (m[:, 0:K] + m[:, K : 2 * K]) + q_buf[rows, :]
            x_buf[rows, :] = jnp.maximum(moved, 0.0)
        return carry

    lax.fori_loop(0, ITER_A, refine, 0)
    out_foot[...] = x_buf[...].astype(BF16)

    drain(packed.at[pl.ds(0, CHIPS - 1)], gram_send)
    drain(msg.at[pl.ds(0, (CHIPS - 1) * SENT)], msg_send)
    drain(back.at[pl.ds(0, (CHIPS - 1) * 3)], back_send)


def body(recording, footprints, slot_owner, slot_pick, traces):
    vmem = pl.BlockSpec(memory_space=pltpu.VMEM)
    dma = pltpu.SemaphoreType.DMA
    return pl.pallas_call(
        kernel,
        out_shape=(
            jax.ShapeDtypeStruct(traces.shape, F32),
            jax.ShapeDtypeStruct(footprints.shape, BF16),
        ),
        in_specs=[pl.BlockSpec(memory_space=pltpu.HBM)] * 5,
        out_specs=(vmem, vmem),
        scratch_shapes=[
            pltpu.VMEM((V, K), BF16),
            pltpu.VMEM((V, K), BF16),
            pltpu.VMEM((1, K), I32),
            pltpu.VMEM((1, K), I32),
            pltpu.VMEM(traces.shape, F32),
            pltpu.VMEM((CHIPS, K, K), BF16),
            pltpu.VMEM((CHIPS, 3 * K // 4, K), BF16),
            pltpu.VMEM((CHIPS * 8, K), F32),
            pltpu.VMEM((CHIPS * 8, K), F32),
            pltpu.VMEM((2, CHIPS, K), F32),
            pltpu.VMEM((ITER_C + 1, 2 * PICKS, K), F32),
            pltpu.VMEM((ITER_C, 2 * PICKS, K), F32),
            pltpu.VMEM((PICKS, K), F32),
            pltpu.VMEM((K, K), F32),
            pltpu.VMEM((PICKS, K), F32),
            pltpu.VMEM((K, K), F32),
            pltpu.VMEM((CHIPS * 4, K), F32),
            pltpu.VMEM((CHIPS * 4, K), F32),
            pltpu.VMEM((XS, K, 2 * K), BF16),
            pltpu.VMEM((XS, V, K), BF16),
            pltpu.VMEM((V, K), F32),
            pltpu.VMEM((V, K), F32),
            pltpu.VMEM((2 * K, 2 * K), BF16),
            pltpu.VMEM((2, CHIPS, K), I32),
            pltpu.VMEM((2, CHIPS, K), I32),
            pltpu.VMEM((CHIPS, K), I32),
            pltpu.VMEM((CHIPS, K), I32),
            pltpu.VMEM((2, 2, CHIPS, K), F32),
            dma,
            dma((RING,)),
            dma((4, 2, RING)),
            dma,
            dma,
            dma((ITER_C + 2,)),
            dma((ITER_C + 2,)),
            dma,
            dma,
            dma((XS,)),
            dma((XS,)),
            dma((XS,)),
            dma((XS,)),
            dma((2,)),
            dma((5,)),
            pltpu.SemaphoreType.REGULAR,
        ],
        compiler_params=pltpu.CompilerParams(
            collective_id=0, has_side_effects=True, vmem_limit_bytes=40 << 20
        ),
    )(recording, footprints, slot_owner.reshape(1, K), slot_pick.reshape(1, K), traces)


def solution(mesh):
    in_specs = (P("tile", "frame"), P("tile", None), P("tile", None), P("tile"), P("tile", "frame"))
    out_specs = (P("tile", "frame"), P("tile", None))
    return jax.shard_map(body, mesh=mesh, in_specs=in_specs, out_specs=out_specs, check_vma=False)
```
